256 devices in a mesh: out: 8 (over z), inp: 32 (over y, x, core).
Axes of the slice: x: 4, y: 4, z: 8, core: 2. Of those that a mesh axis runs over, the one named last changes fastest.
Arguments:
- weight_delta: bfloat16 [8192, 38912], P('inp', 'out'), may hold values from -6 to 6
- resident: bfloat16 [38912, 8192], P(('out', 'inp')), may hold values from -6 to 6
Outputs:
- refreshed: bfloat16 [38912, 8192], P(('out', 'inp'))
The draws below stay inside these ranges and needn't reach their ends.
All inputs are finite; a program needn't handle non-finite values.
Results may differ from the reference program's by a relative error of at most 0.001.
Values may be sent and summed in bfloat16 or wider, within the bound.
A program may use at most 64 MiB of HBM per device.

```python
import jax
import jax.numpy as jnp
from jax import lax

IN = 8192
COLS = 38912
N_OUT = 8
N_INP = 32


def level_of(key, shape, cuts, low, largest):
    loudness = 1.0
    for position, blocks in cuts:
        draws = jax.random.uniform(jax.random.fold_in(jax.random.fold_in(key, 6), position), (blocks,), jnp.float32, low / len(cuts), largest / len(cuts))
        loudness = loudness * jnp.repeat(jnp.exp(draws), shape[position] // blocks).reshape((-1,) + (1,) * (len(shape) - 1 - position))
    return loudness


def noise(rng, extent, spread, most, pieces=(), dtype=jnp.bfloat16):
    drawn = jax.random.normal(rng, extent, jnp.float32) * spread
    if len(pieces) > 0:
        drawn = level_of(rng, extent, pieces, -0.22, 0.18) * drawn
    return jnp.clip(drawn, min=-most, max=most).astype(dtype)


def setup_inputs(seed: int = 0) -> dict:
    key_list = jax.random.split(jax.random.key(seed), 3)
    return {
        "weight_delta": noise(key_list[0], (IN, COLS), 1.0, 6.0, ((0, 32), (1, 8))),
        "resident": noise(key_list[1], (COLS, IN), 1.0, 6.0, ((0, 256),)),
    }


def walsh_section(column_block):
    rows_total = column_block.shape[0]
    stride = 1
    current = column_block
    while stride < rows_total:
        shaped = current.reshape(rows_total // (2 * stride), 2, stride, -1)
        first_half = shaped[:, 0]
        second_half = shaped[:, 1]
        current = jnp.stack([first_half + second_half, first_half - second_half], axis=1).reshape(rows_total, -1)
        stride = stride * 2
    return current

def reference(weight_delta, resident):
    groups = N_OUT * N_INP
    block_cols = COLS // groups
    factor = 1.0 / jnp.sqrt(jnp.float32(IN))
    delta_blocks = weight_delta.reshape(IN, groups, block_cols).transpose(1, 0, 2)
    resident_blocks = resident.reshape(groups, block_cols, IN)

    def one_block(pair):
        delta_block, resident_block = pair
        rotated = walsh_section(delta_block.astype(jnp.float32)) * factor
        return (resident_block.astype(jnp.float32) + rotated.T).astype(jnp.bfloat16)
    refreshed = lax.map(one_block, (delta_blocks, resident_blocks))
    return refreshed.reshape(COLS, IN)
```

```python
import functools

import jax
import jax.numpy as jnp
from jax import lax
from jax.experimental import pallas as pl
from jax.experimental.pallas import tpu as pltpu
from jax.sharding import PartitionSpec as P

LANES = 128
SIDE = 4
CORES = 2
CHUNK = 16
FAR_A = ((2, 0), (3, 1))
FAR_B = ((0, 1), (3, 2))
MESH = pl.DeviceIdType.MESH
def sylvester(order):
    rows = lax.broadcasted_iota(jnp.int32, (order, order), 0)
    cols = lax.broadcasted_iota(jnp.int32, (order, order), 1)
    parity = rows & cols
    for shift in (4, 2, 1):
        parity = parity ^ (parity >> shift)
    return (1 - 2 * (parity & 1)).astype(jnp.float32).astype(jnp.bfloat16)


def selection(order, window, shift):
    rows = lax.broadcasted_iota(jnp.int32, (order, window), 0)
    cols = lax.broadcasted_iota(jnp.int32, (order, window), 1)
    return jnp.where(cols == rows + shift, 1.0, 0.0).astype(jnp.bfloat16)


def butterfly(values):
    values = list(values)
    stride = 1
    while stride < len(values):
        for at in range(len(values)):
            if at & stride == 0:
                first, second = values[at], values[at + stride]
                values[at], values[at + stride] = first + second, first - second
        stride *= 2
    return values


def exchange_kernel(
    update_hbm, work_ref, update, sending, middle, relay, received,
    load_sem, send_sems, middle_sems, relay_sems, recv_sems,
):
    cols = update.shape[1]
    stacked = received.shape[1]
    feats = stacked // 2
    groups = cols // feats
    window = -(-(CORES * feats + LANES - 1) // LANES) * LANES
    me = lax.axis_index("inp")
    core = me % CORES
    my_chip = me // CORES
    my_x = my_chip % SIDE
    my_y = my_chip // SIDE
    my_a = my_x + core * (my_y - my_x)
    my_b = my_y + core * (my_x - my_y)

    def chip_at(da, db):
        a, b = (my_a + da) % SIDE, (my_b + db) % SIDE
        x, y = a + core * (b - a), b + core * (a - b)
        return y * SIDE + x

    def device_at(da, db, c):
        return chip_at(da, db) * CORES + c

    load = pltpu.make_async_copy(update_hbm, update, load_sem)
    load.start()
    barrier = pltpu.get_barrier_semaphore()
    others = [device_at(da, db, c) for da, db in ((1, 0), (3, 0), (0, 1), (0, 3)) for c in range(CORES)]
    others.append(device_at(0, 0, 1 - core))
    for device in others:
        pl.semaphore_signal(barrier, inc=1, device_id={"inp": device}, device_id_type=MESH)

    def make(da, db):
        chip = chip_at(da, db)
        first = jnp.minimum(chip * CORES * feats // LANES, (cols - window) // LANES)
        shift = chip * CORES * feats - first * LANES
        columns = update[:, pl.ds(pl.multiple_of(first * LANES, LANES), window)]
        turned = lax.dot_general(
            selection(CORES * feats, window, shift), columns, (((1,), (1,)), ((), ())),
            preferred_element_type=jnp.float32,
        )
        for c in range(CORES):
            rows = turned[c * feats : (c + 1) * feats]
            sending[da, db, c] = jnp.concatenate([rows[:, :LANES], rows[:, LANES:]], axis=0).astype(sending.dtype)

    sends = []

    def send(src, dst, sem, device):
        copy = pltpu.make_async_remote_copy(
            src_ref=src, dst_ref=dst, send_sem=send_sems.at[len(sends)], recv_sem=sem,
            device_id={"inp": device}, device_id_type=MESH,
        )
        copy.start()
        sends.append(copy)

    def wait(dst, sem):
        pltpu.make_async_remote_copy(
            src_ref=dst, dst_ref=dst, send_sem=send_sems.at[0], recv_sem=sem,
            device_id={"inp": me}, device_id_type=MESH,
        ).wait_recv()

    def held(da, db):
        return sending.at[da, db] if da == 0 else middle.at[da, db]

    def to_middle(src, step, da, db):
        send(src, middle.at[da, db], middle_sems.at[da, db], device_at(step, 0, core))

    def to_relay(src, step, way, slot):
        da, db = (step, 0) if way < 2 else (0, step)
        send(src, relay.at[way, slot], relay_sems.at[way, slot], device_at(da, db, core))

    def to_end(src, step, da, db):
        source = device_at(SIDE - da, db, core)
        for c in range(CORES):
            send(src.at[c], received.at[source], recv_sems.at[source], device_at(0, step, c))

    def wait_middle(da, db):
        wait(middle.at[da, db], middle_sems.at[da, db])

    def hand_on(way, slot):
        wait(relay.at[way, slot], relay_sems.at[way, slot])
        step = (1, 3)[way % 2]
        if way < 2:
            to_middle(relay.at[way, slot], step, 2, FAR_A[way][slot])
        else:
            to_end(relay.at[way, slot], step, FAR_B[way - 2][slot], SIDE - step)

    def home(da):
        block = held(da, 0)
        source = device_at(SIDE - da, 0, core)
        send(block.at[1 - core], received.at[source], recv_sems.at[source], device_at(0, 0, 1 - core))
        received[source] = block[core]

    load.wait()
    for way in range(2):
        make(2, FAR_A[way][0])
    pl.semaphore_wait(barrier, len(others))

    for slot in range(2):
        for way in range(2):
            db = FAR_A[way][slot]
            if slot > 0:
                make(2, db)
            to_relay(sending.at[2, db], (1, 3)[way], way, slot)

    def along(db):
        for da in (1, 3):
            make(da, db)
            to_middle(sending.at[da, db], da, da, db)

    along(2)
    along(1)
    hand_on(0, 0)
    hand_on(1, 0)
    along(3)
    hand_on(0, 1)
    hand_on(1, 1)
    along(0)

    make(0, 2)
    to_relay(held(0, 2), 1, 2, 0)
    wait_middle(3, 2)
    to_relay(held(3, 2), 3, 3, 0)
    wait_middle(1, 2)
    to_relay(held(1, 2), 1, 2, 1)
    for db in (1, 3):
        make(0, db)
        to_end(held(0, db), db, 0, 0)
    wait_middle(2, 2)
    to_relay(held(2, 2), 3, 3, 1)
    for da in (1, 3):
        for db in (1, 3):
            wait_middle(da, db)
            to_end(held(da, db), db, da, 0)
    make(0, 0)
    home(0)
    hand_on(2, 0)
    hand_on(3, 0)
    for db in (1, 3):
        wait_middle(2, db)
        to_end(held(2, db), db, 2, 0)
    for da in (1, 3, 2):
        wait_middle(da, 0)
        home(da)
    hand_on(2, 1)
    hand_on(3, 1)

    matrix = sylvester(LANES)
    for da, db in ((0, 0), (1, 0), (3, 0), (2, 0), (0, 1), (0, 3), (1, 1), (3, 3), (1, 3), (3, 1),
                   (0, 2), (2, 1), (2, 3), (1, 2), (3, 2), (2, 2)):
        from_x, from_y = (my_x + da) % SIDE, (my_y + db) % SIDE
        chip = from_y * SIDE + from_x
        for c in range(CORES):
            if (db, da)[c] == 0:

                @pl.when(core != c)
                def _(source=chip * CORES + c):
                    wait(received.at[source], recv_sems.at[source])
            else:
                wait(received.at[chip * CORES + c], recv_sems.at[chip * CORES + c])
        parts = []
        for c in range(CORES):
            both = jnp.dot(received[chip * CORES + c], matrix, preferred_element_type=jnp.float32)
            parts += [both[:feats], both[feats:]]
        for at, value in enumerate(butterfly(parts)):
            work_ref[from_y, from_x, at] = value

    for copy in sends:
        copy.wait_send()


def finish_kernel(work_ref, resident, out_hbm, out, out_sems):
    feats, width = out.shape
    factor = 1.0 / jnp.sqrt(jnp.float32(width))
    whole = feats // CHUNK

    def store(chunk, rows):
        return pltpu.make_async_copy(out.at[rows], out_hbm.at[rows], out_sems.at[chunk])

    def finish(rows):
        for at in range(2 * CORES):
            values = butterfly([work_ref[y, x, at, rows, :] for y in range(SIDE) for x in range(SIDE)])
            for chip, value in enumerate(values):
                cols = pl.ds((chip * 2 * CORES + at) * LANES, LANES)
                total = resident[rows, cols].astype(jnp.float32) + value * factor
                out[rows, cols] = total.astype(out.dtype)

    @pl.loop(0, whole)
    def _(chunk):
        rows = pl.ds(pl.multiple_of(chunk * CHUNK, CHUNK), CHUNK)
        finish(rows)
        store(chunk, rows).start()

    rest = pl.ds(whole * CHUNK, feats % CHUNK)
    if feats % CHUNK:
        finish(rest)
        store(whole, rest).start()
        store(whole, rest).wait()

    @pl.loop(0, whole)
    def _(chunk):
        store(chunk, pl.ds(pl.multiple_of(chunk * CHUNK, CHUNK), CHUNK)).wait()


def shards(weight_delta, resident):
    rows, cols = weight_delta.shape
    groups = lax.axis_size("inp")
    feats = cols // groups
    size = rows * cols
    work = pl.pallas_call(
        exchange_kernel,
        out_shape=pltpu.VMEM((SIDE, SIDE, 2 * CORES, feats, LANES), jnp.float32),
        in_specs=[pl.BlockSpec(memory_space=pl.ANY)],
        out_specs=pl.BlockSpec(memory_space=pltpu.VMEM),
        scratch_shapes=[
            pltpu.VMEM((rows, cols), weight_delta.dtype),
            pltpu.VMEM((SIDE, SIDE, CORES, 2 * feats, LANES), weight_delta.dtype),
            pltpu.VMEM((SIDE, SIDE, CORES, 2 * feats, LANES), weight_delta.dtype),
            pltpu.VMEM((4, 2, CORES, 2 * feats, LANES), weight_delta.dtype),
            pltpu.VMEM((groups, 2 * feats, LANES), weight_delta.dtype),
            pltpu.SemaphoreType.DMA,
            pltpu.SemaphoreType.DMA((64,)),
            pltpu.SemaphoreType.DMA((SIDE, SIDE)),
            pltpu.SemaphoreType.DMA((4, 2)),
            pltpu.SemaphoreType.DMA((groups,)),
        ],
        compiler_params=pltpu.CompilerParams(
            collective_id=0, has_side_effects=True, vmem_limit_bytes=32 * 1024 * 1024
        ),
        cost_estimate=pl.CostEstimate(flops=2 * size * (rows + LANES), bytes_accessed=2 * size, transcendentals=0),
    )(pltpu.with_memory_space_constraint(weight_delta, pltpu.HBM))
    return pl.pallas_call(
        finish_kernel,
        out_shape=jax.ShapeDtypeStruct(resident.shape, resident.dtype),
        in_specs=[pl.BlockSpec(memory_space=pltpu.VMEM)] * 2,
        out_specs=pl.BlockSpec(memory_space=pl.ANY),
        scratch_shapes=[
            pltpu.VMEM(resident.shape, resident.dtype),
            pltpu.SemaphoreType.DMA((-(-feats // CHUNK),)),
        ],
        compiler_params=pltpu.CompilerParams(vmem_limit_bytes=32 * 1024 * 1024),
        cost_estimate=pl.CostEstimate(flops=6 * size, bytes_accessed=4 * size, transcendentals=0),
    )(work, resident)


def solution(mesh):
    placed = (P("inp", "out"), P(("out", "inp"), None))
    return jax.shard_map(
        shards, mesh=mesh, in_specs=placed, out_specs=P(("out", "inp"), None), check_vma=False
    )
```

```python
import functools

import jax
import jax.numpy as jnp
from jax import lax
from jax.experimental import pallas as pl
from jax.experimental.pallas import tpu as pltpu
from jax.sharding import PartitionSpec as P

LANES = 128
SIDE = 4
CORES = 2
CHUNK = 16
FAR_A = ((2, 0), (3, 1))
FAR_B = ((0, 1), (3, 2))
ARRIVALS = (
    (0, 0), (1, 0), (3, 0), (2, 0), (0, 2), (1, 1), (3, 1), (3, 2),
    (1, 2), (1, 3), (3, 3), (2, 2), (2, 3), (2, 1), (0, 1), (0, 3),
)
MESH = pl.DeviceIdType.MESH
def window_of(feats):
    return -(-(CORES * feats + LANES - 1) // LANES) * LANES


def sylvester(order):
    rows = lax.broadcasted_iota(jnp.int32, (order, order), 0)
    cols = lax.broadcasted_iota(jnp.int32, (order, order), 1)
    parity = rows & cols
    for shift in (4, 2, 1):
        parity = parity ^ (parity >> shift)
    return (1 - 2 * (parity & 1)).astype(jnp.float32).astype(jnp.bfloat16)


def selection(order, window, shift):
    rows = lax.broadcasted_iota(jnp.int32, (order, window), 0)
    cols = lax.broadcasted_iota(jnp.int32, (order, window), 1)
    return jnp.where(cols == rows + shift, 1.0, 0.0).astype(jnp.bfloat16)


def butterfly(values):
    values = list(values)
    stride = 1
    while stride < len(values):
        for at in range(len(values)):
            if at & stride == 0:
                first, second = values[at], values[at + stride]
                values[at], values[at + stride] = first + second, first - second
        stride *= 2
    return values


def exchange_kernel(
    update_hbm, work_ref, update, early, sending, middle, relay, received,
    load_sem, early_sems, send_sems, middle_sems, relay_sems, recv_sems,
):
    cols = update.shape[1]
    stacked = received.shape[1]
    feats = stacked // 2
    groups = cols // feats
    window = window_of(feats)
    me = lax.axis_index("inp")
    core = me % CORES
    my_chip = me // CORES
    my_x = my_chip % SIDE
    my_y = my_chip // SIDE
    my_a = my_x + core * (my_y - my_x)
    my_b = my_y + core * (my_x - my_y)

    def chip_at(da, db):
        a, b = (my_a + da) % SIDE, (my_b + db) % SIDE
        x, y = a + core * (b - a), b + core * (a - b)
        return y * SIDE + x

    def device_at(da, db, c):
        return chip_at(da, db) * CORES + c

    def window_at(da, db):
        chip = chip_at(da, db)
        first = jnp.minimum(chip * CORES * feats // LANES, (cols - window) // LANES)
        return pl.ds(pl.multiple_of(first * LANES, LANES), window), chip * CORES * feats - first * LANES

    firsts = [
        pltpu.make_async_copy(update_hbm.at[:, window_at(2, FAR_A[way][0])[0]], early.at[way], early_sems.at[way])
        for way in range(2)
    ]
    load = pltpu.make_async_copy(update_hbm, update, load_sem)
    for copy in (*firsts, load):
        copy.start()
    barrier = pltpu.get_barrier_semaphore()
    others = [device_at(da, db, c) for da, db in ((1, 0), (3, 0), (0, 1), (0, 3)) for c in range(CORES)]
    others.append(device_at(0, 0, 1 - core))
    for device in others:
        pl.semaphore_signal(barrier, inc=1, device_id={"inp": device}, device_id_type=MESH)

    def make(da, db, columns=None):
        at, shift = window_at(da, db)
        turned = lax.dot_general(
            selection(CORES * feats, window, shift),
            update[:, at] if columns is None else columns,
            (((1,), (1,)), ((), ())),
            preferred_element_type=jnp.float32,
        )
        for c in range(CORES):
            rows = turned[c * feats : (c + 1) * feats]
            sending[da, db, c] = jnp.concatenate([rows[:, :LANES], rows[:, LANES:]], axis=0).astype(sending.dtype)

    sends = []

    def send(src, dst, sem, device):
        copy = pltpu.make_async_remote_copy(
            src_ref=src, dst_ref=dst, send_sem=send_sems.at[len(sends)], recv_sem=sem,
            device_id={"inp": device}, device_id_type=MESH,
        )
        copy.start()
        sends.append(copy)

    def wait(dst, sem):
        pltpu.make_async_remote_copy(
            src_ref=dst, dst_ref=dst, send_sem=send_sems.at[0], recv_sem=sem,
            device_id={"inp": me}, device_id_type=MESH,
        ).wait_recv()

    def held(da, db):
        return sending.at[da, db] if da == 0 else middle.at[da, db]

    def wait_held(da, db):
        if da != 0:
            wait(middle.at[da, db], middle_sems.at[da, db])

    def to_middle(src, step, da, db):
        send(src, middle.at[da, db], middle_sems.at[da, db], device_at(step, 0, core))

    def to_relay(src, way, slot):
        step = (1, 3)[way % 2]
        da, db = (step, 0) if way < 2 else (0, step)
        send(src, relay.at[way, slot], relay_sems.at[way, slot], device_at(da, db, core))

    def to_end(src, step, da, db):
        source = device_at(SIDE - da, db, core)
        for c in range(CORES):
            send(src.at[c], received.at[source], recv_sems.at[source], device_at(0, step, c))

    def far_a(slot):
        for way in range(2):
            to_relay(sending.at[2, FAR_A[way][slot]], way, slot)

    def near_a(db):
        for da in (1, 3):
            make(da, db)
        for da in (1, 3):
            to_middle(sending.at[da, db], da, da, db)

    def far_b(way, slot):
        da = FAR_B[way - 2][slot]
        wait_held(da, 2)
        to_relay(held(da, 2), way, slot)

    def near_b(da, db):
        wait_held(da, db)
        to_end(held(da, db), db, da, 0)

    def hand_on(way, slot):
        wait(relay.at[way, slot], relay_sems.at[way, slot])
        step = (1, 3)[way % 2]
        if way < 2:
            to_middle(relay.at[way, slot], step, 2, FAR_A[way][slot])
        else:
            to_end(relay.at[way, slot], step, FAR_B[way - 2][slot], SIDE - step)

    def home(da):
        wait_held(da, 0)
        block = held(da, 0)
        source = device_at(SIDE - da, 0, core)
        send(block.at[1 - core], received.at[source], recv_sems.at[source], device_at(0, 0, 1 - core))
        received[source] = block[core]

    for way in range(2):
        firsts[way].wait()
        make(2, FAR_A[way][0], early[way])
    pl.semaphore_wait(barrier, len(others))

    far_a(0)
    load.wait()
    make(0, 2)
    far_b(2, 0)
    near_a(2)
    for way in range(2):
        make(2, FAR_A[way][1])
    far_a(1)
    hand_on(0, 0)
    hand_on(1, 0)
    near_a(1)
    far_b(3, 0)
    far_b(2, 1)
    near_a(3)
    hand_on(0, 1)
    hand_on(1, 1)
    far_b(3, 1)
    hand_on(2, 0)
    near_a(0)
    near_b(1, 1)
    near_b(3, 1)
    hand_on(3, 0)
    hand_on(2, 1)
    near_b(1, 3)
    near_b(3, 3)
    hand_on(3, 1)
    near_b(2, 3)
    near_b(2, 1)
    make(0, 1)
    make(0, 3)
    near_b(0, 1)
    near_b(0, 3)
    make(0, 0)
    for da in (0, 1, 3, 2):
        home(da)

    matrix = sylvester(LANES)

    def rotate(da, db, c):
        x, y = (da, db)[c], (db, da)[c]
        from_x, from_y = (my_x + SIDE - x) % SIDE, (my_y + SIDE - y) % SIDE
        source = (from_y * SIDE + from_x) * CORES + c
        if db == 0:
            @pl.when(core != c)
            def _():
                wait(received.at[source], recv_sems.at[source])
        else:
            wait(received.at[source], recv_sems.at[source])
        both = jnp.dot(received[source], matrix, preferred_element_type=jnp.float32)
        halves = both[:feats] + both[feats:], both[:feats] - both[feats:]
        if ARRIVALS.index((da, db)) < ARRIVALS.index((db, da)) or (da == db and c == 0):
            for half in range(2):
                work_ref[from_y, from_x, 2 * c + half] = halves[half]
        else:
            for half in range(2):
                there = work_ref[from_y, from_x, 2 * (1 - c) + half]
                work_ref[from_y, from_x, half] = halves[half] + there
                work_ref[from_y, from_x, 2 + half] = halves[half] - there if c == 0 else there - halves[half]

    for da, db in ARRIVALS:
        for c in range(CORES):
            rotate(da, db, c)

    for copy in sends:
        copy.wait_send()


def finish_kernel(work_ref, resident, out_hbm, out, out_sems):
    feats, width = out.shape
    factor = 1.0 / jnp.sqrt(jnp.float32(width))
    whole = feats // CHUNK

    def store(chunk, rows):
        return pltpu.make_async_copy(out.at[rows], out_hbm.at[rows], out_sems.at[chunk])

    def finish(rows):
        for at in range(2 * CORES):
            values = butterfly([work_ref[y, x, at, rows, :] for y in range(SIDE) for x in range(SIDE)])
            for chip, value in enumerate(values):
                cols = pl.ds((chip * 2 * CORES + at) * LANES, LANES)
                total = resident[rows, cols].astype(jnp.float32) + value * factor
                out[rows, cols] = total.astype(out.dtype)

    @pl.loop(0, whole)
    def _(chunk):
        rows = pl.ds(pl.multiple_of(chunk * CHUNK, CHUNK), CHUNK)
        finish(rows)
        store(chunk, rows).start()

    rest = pl.ds(whole * CHUNK, feats % CHUNK)
    if feats % CHUNK:
        finish(rest)
        store(whole, rest).start()
        store(whole, rest).wait()

    @pl.loop(0, whole)
    def _(chunk):
        store(chunk, pl.ds(pl.multiple_of(chunk * CHUNK, CHUNK), CHUNK)).wait()


def shards(weight_delta, resident):
    rows, cols = weight_delta.shape
    groups = lax.axis_size("inp")
    feats = cols // groups
    size = rows * cols
    work = pl.pallas_call(
        exchange_kernel,
        out_shape=pltpu.VMEM((SIDE, SIDE, 2 * CORES, feats, LANES), jnp.float32),
        in_specs=[pl.BlockSpec(memory_space=pl.ANY)],
        out_specs=pl.BlockSpec(memory_space=pltpu.VMEM),
        scratch_shapes=[
            pltpu.VMEM((rows, cols), weight_delta.dtype),
            pltpu.VMEM((2, rows, window_of(feats)), weight_delta.dtype),
            pltpu.VMEM((SIDE, SIDE, CORES, 2 * feats, LANES), weight_delta.dtype),
            pltpu.VMEM((SIDE, SIDE, CORES, 2 * feats, LANES), weight_delta.dtype),
            pltpu.VMEM((4, 2, CORES, 2 * feats, LANES), weight_delta.dtype),
            pltpu.VMEM((groups, 2 * feats, LANES), weight_delta.dtype),
            pltpu.SemaphoreType.DMA,
            pltpu.SemaphoreType.DMA((2,)),
            pltpu.SemaphoreType.DMA((64,)),
            pltpu.SemaphoreType.DMA((SIDE, SIDE)),
            pltpu.SemaphoreType.DMA((4, 2)),
            pltpu.SemaphoreType.DMA((groups,)),
        ],
        compiler_params=pltpu.CompilerParams(
            collective_id=0, has_side_effects=True, vmem_limit_bytes=32 * 1024 * 1024
        ),
        cost_estimate=pl.CostEstimate(flops=2 * size * (rows + LANES), bytes_accessed=2 * size, transcendentals=0),
    )(pltpu.with_memory_space_constraint(weight_delta, pltpu.HBM))
    return pl.pallas_call(
        finish_kernel,
        out_shape=jax.ShapeDtypeStruct(resident.shape, resident.dtype),
        in_specs=[pl.BlockSpec(memory_space=pltpu.VMEM)] * 2,
        out_specs=pl.BlockSpec(memory_space=pl.ANY),
        scratch_shapes=[
            pltpu.VMEM(resident.shape, resident.dtype),
            pltpu.SemaphoreType.DMA((-(-feats // CHUNK),)),
        ],
        compiler_params=pltpu.CompilerParams(vmem_limit_bytes=32 * 1024 * 1024),
        cost_estimate=pl.CostEstimate(flops=6 * size, bytes_accessed=4 * size, transcendentals=0),
    )(work, resident)


def solution(mesh):
    placed = (P("inp", "out"), P(("out", "inp"), None))
    return jax.shard_map(
        shards, mesh=mesh, in_specs=placed, out_specs=P(("out", "inp"), None), check_vma=False
    )
```

```python
import functools

import jax
import jax.numpy as jnp
from jax import lax
from jax.experimental import pallas as pl
from jax.experimental.pallas import tpu as pltpu
from jax.sharding import PartitionSpec as P

LANES = 128
SIDE = 4
CORES = 2
CHUNK = 16
FAR_A = ((2, 0), (3, 1))
FAR_B = ((0, 1), (3, 2))
ARRIVALS = (
    (0, 0), (1, 0), (3, 0), (2, 0), (0, 1), (0, 3), (1, 1), (1, 3),
    (3, 1), (3, 3), (0, 2), (3, 2), (2, 1), (2, 3), (1, 2), (2, 2),
)

MESH = pl.DeviceIdType.MESH


def window_of(feats):
    return -(-(CORES * feats + LANES - 1) // LANES) * LANES


def sylvester(order):
    rows = lax.broadcasted_iota(jnp.int32, (order, order), 0)
    cols = lax.broadcasted_iota(jnp.int32, (order, order), 1)
    parity = rows & cols
    for shift in (4, 2, 1):
        parity = parity ^ (parity >> shift)
    return (1 - 2 * (parity & 1)).astype(jnp.float32).astype(jnp.bfloat16)


def selection(order, window, shift):
    rows = lax.broadcasted_iota(jnp.int32, (order, window), 0)
    cols = lax.broadcasted_iota(jnp.int32, (order, window), 1)
    return jnp.where(cols == rows + shift, 1.0, 0.0).astype(jnp.bfloat16)


def butterfly(values):
    values = list(values)
    stride = 1
    while stride < len(values):
        for at in range(len(values)):
            if at & stride == 0:
                first, second = values[at], values[at + stride]
                values[at], values[at + stride] = first + second, first - second
        stride *= 2
    return values


def exchange_kernel(
    update_hbm, work_ref, update, early, sending, middle, relay, received,
    load_sem, early_sems, send_sems, middle_sems, relay_sems, recv_sems,
):
    cols = update.shape[1]
    stacked = received.shape[1]
    feats = stacked // 2
    groups = cols // feats
    window = window_of(feats)
    me = lax.axis_index("inp")
    core = me % CORES
    my_chip = me // CORES
    my_x = my_chip % SIDE
    my_y = my_chip // SIDE
    my_a = my_x + core * (my_y - my_x)
    my_b = my_y + core * (my_x - my_y)

    def chip_at(da, db):
        a, b = (my_a + da) % SIDE, (my_b + db) % SIDE
        x, y = a + core * (b - a), b + core * (a - b)
        return y * SIDE + x

    def device_at(da, db, c):
        return chip_at(da, db) * CORES + c

    def window_at(da, db):
        chip = chip_at(da, db)
        first = jnp.minimum(chip * CORES * feats // LANES, (cols - window) // LANES)
        return pl.ds(pl.multiple_of(first * LANES, LANES), window), chip * CORES * feats - first * LANES

    firsts = [
        pltpu.make_async_copy(update_hbm.at[:, window_at(2, FAR_A[way][0])[0]], early.at[way], early_sems.at[way])
        for way in range(2)
    ]
    load = pltpu.make_async_copy(update_hbm, update, load_sem)
    for copy in (*firsts, load):
        copy.start()
    barrier = pltpu.get_barrier_semaphore()
    others = [device_at(da, db, c) for da, db in ((1, 0), (3, 0), (0, 1), (0, 3)) for c in range(CORES)]
    others.append(device_at(0, 0, 1 - core))
    for device in others:
        pl.semaphore_signal(barrier, inc=1, device_id={"inp": device}, device_id_type=MESH)

    def make(da, db, columns=None):
        at, shift = window_at(da, db)
        turned = lax.dot_general(
            selection(CORES * feats, window, shift),
            update[:, at] if columns is None else columns,
            (((1,), (1,)), ((), ())),
            preferred_element_type=jnp.float32,
        )
        for c in range(CORES):
            rows = turned[c * feats : (c + 1) * feats]
            sending[da, db, c] = jnp.concatenate([rows[:, :LANES], rows[:, LANES:]], axis=0).astype(sending.dtype)

    sends = []

    def send(src, dst, sem, device):
        copy = pltpu.make_async_remote_copy(
            src_ref=src, dst_ref=dst, send_sem=send_sems.at[len(sends)], recv_sem=sem,
            device_id={"inp": device}, device_id_type=MESH,
        )
        copy.start()
        sends.append(copy)

    def wait(dst, sem):
        pltpu.make_async_remote_copy(
            src_ref=dst, dst_ref=dst, send_sem=send_sems.at[0], recv_sem=sem,
            device_id={"inp": me}, device_id_type=MESH,
        ).wait_recv()

    def held(da, db):
        return sending.at[da, db] if da == 0 else middle.at[da, db]

    def wait_held(da, db):
        if da != 0:
            wait(middle.at[da, db], middle_sems.at[da, db])

    def to_middle(src, step, da, db):
        send(src, middle.at[da, db], middle_sems.at[da, db], device_at(step, 0, core))

    def to_relay(src, way, slot):
        step = (1, 3)[way % 2]
        da, db = (step, 0) if way < 2 else (0, step)
        send(src, relay.at[way, slot], relay_sems.at[way, slot], device_at(da, db, core))

    def to_ends(blocks):
        for c in range(CORES):
            for src, step, da, db in blocks:
                source = device_at(SIDE - da, db, core)
                send(src.at[c], received.at[source], recv_sems.at[source], device_at(0, step, c))

    def far_a(slot):
        for way in range(2):
            to_relay(sending.at[2, FAR_A[way][slot]], way, slot)

    def near_a(db):
        for da in (1, 3):
            make(da, db)
        for da in (1, 3):
            to_middle(sending.at[da, db], da, da, db)

    def far_b(slot):
        for way in (2, 3):
            wait_held(FAR_B[way - 2][slot], 2)
        for way in (2, 3):
            to_relay(held(FAR_B[way - 2][slot], 2), way, slot)

    def near_b(da):
        for db in (1, 3):
            wait_held(da, db)
        to_ends([(held(da, db), db, da, 0) for db in (1, 3)])

    def on_a(slot):
        for way in range(2):
            wait(relay.at[way, slot], relay_sems.at[way, slot])
            to_middle(relay.at[way, slot], (1, 3)[way], 2, FAR_A[way][slot])

    def on_b(slot):
        for way in (2, 3):
            wait(relay.at[way, slot], relay_sems.at[way, slot])
        to_ends([(relay.at[way, slot], step, FAR_B[way - 2][slot], SIDE - step) for way, step in ((2, 1), (3, 3))])

    def home(da):
        wait_held(da, 0)
        block = held(da, 0)
        source = device_at(SIDE - da, 0, core)
        send(block.at[1 - core], received.at[source], recv_sems.at[source], device_at(0, 0, 1 - core))
        received[source] = block[core]

    for way in range(2):
        firsts[way].wait()
        make(2, FAR_A[way][0], early[way])
    pl.semaphore_wait(barrier, len(others))

    far_a(0)
    load.wait()
    for way in range(2):
        make(2, FAR_A[way][1])
    far_a(1)
    near_a(2)
    near_a(1)
    on_a(0)
    near_a(3)
    on_a(1)
    near_a(0)

    make(0, 2)
    far_b(0)
    make(0, 1)
    make(0, 3)
    near_b(0)
    far_b(1)
    near_b(1)
    near_b(3)
    make(0, 0)
    home(0)
    on_b(0)
    near_b(2)
    for da in (1, 3, 2):
        home(da)
    on_b(1)

    matrix = sylvester(LANES)

    def rotate(da, db, c):
        x, y = (da, db)[c], (db, da)[c]
        from_x, from_y = (my_x + SIDE - x) % SIDE, (my_y + SIDE - y) % SIDE
        source = (from_y * SIDE + from_x) * CORES + c
        if db == 0:
            @pl.when(core != c)
            def _():
                wait(received.at[source], recv_sems.at[source])
        else:
            wait(received.at[source], recv_sems.at[source])
        both = jnp.dot(received[source], matrix, preferred_element_type=jnp.float32)
        halves = both[:feats] + both[feats:], both[:feats] - both[feats:]
        if ARRIVALS.index((da, db)) < ARRIVALS.index((db, da)) or (da == db and c == 0):
            for half in range(2):
                work_ref[from_y, from_x, 2 * c + half] = halves[half]
        else:
            for half in range(2):
                there = work_ref[from_y, from_x, 2 * (1 - c) + half]
                work_ref[from_y, from_x, half] = halves[half] + there
                work_ref[from_y, from_x, 2 + half] = halves[half] - there if c == 0 else there - halves[half]

    for da, db in ARRIVALS:
        for c in range(CORES):
            rotate(da, db, c)

    for copy in sends:
        copy.wait_send()


def finish_kernel(work_ref, resident, out_hbm, out, out_sems):
    feats, width = out.shape
    factor = 1.0 / jnp.sqrt(jnp.float32(width))
    whole = feats // CHUNK

    def store(chunk, rows):
        return pltpu.make_async_copy(out.at[rows], out_hbm.at[rows], out_sems.at[chunk])

    def finish(rows):
        for at in range(2 * CORES):
            values = butterfly([work_ref[y, x, at, rows, :] for y in range(SIDE) for x in range(SIDE)])
            for chip, value in enumerate(values):
                cols = pl.ds((chip * 2 * CORES + at) * LANES, LANES)
                total = resident[rows, cols].astype(jnp.float32) + value * factor
                out[rows, cols] = total.astype(out.dtype)

    @pl.loop(0, whole)
    def _(chunk):
        rows = pl.ds(pl.multiple_of(chunk * CHUNK, CHUNK), CHUNK)
        finish(rows)
        store(chunk, rows).start()

    rest = pl.ds(whole * CHUNK, feats % CHUNK)
    if feats % CHUNK:
        finish(rest)
        store(whole, rest).start()
        store(whole, rest).wait()

    @pl.loop(0, whole)
    def _(chunk):
        store(chunk, pl.ds(pl.multiple_of(chunk * CHUNK, CHUNK), CHUNK)).wait()


def shards(weight_delta, resident):
    rows, cols = weight_delta.shape
    groups = lax.axis_size("inp")
    feats = cols // groups
    size = rows * cols
    work = pl.pallas_call(
        exchange_kernel,
        out_shape=pltpu.VMEM((SIDE, SIDE, 2 * CORES, feats, LANES), jnp.float32),
        in_specs=[pl.BlockSpec(memory_space=pl.ANY)],
        out_specs=pl.BlockSpec(memory_space=pltpu.VMEM),
        scratch_shapes=[
            pltpu.VMEM((rows, cols), weight_delta.dtype),
            pltpu.VMEM((2, rows, window_of(feats)), weight_delta.dtype),
            pltpu.VMEM((SIDE, SIDE, CORES, 2 * feats, LANES), weight_delta.dtype),
            pltpu.VMEM((SIDE, SIDE, CORES, 2 * feats, LANES), weight_delta.dtype),
            pltpu.VMEM((4, 2, CORES, 2 * feats, LANES), weight_delta.dtype),
            pltpu.VMEM((groups, 2 * feats, LANES), weight_delta.dtype),
            pltpu.SemaphoreType.DMA,
            pltpu.SemaphoreType.DMA((2,)),
            pltpu.SemaphoreType.DMA((64,)),
            pltpu.SemaphoreType.DMA((SIDE, SIDE)),
            pltpu.SemaphoreType.DMA((4, 2)),
            pltpu.SemaphoreType.DMA((groups,)),
        ],
        compiler_params=pltpu.CompilerParams(
            collective_id=0, has_side_effects=True, vmem_limit_bytes=32 * 1024 * 1024
        ),
        cost_estimate=pl.CostEstimate(flops=2 * size * (rows + LANES), bytes_accessed=2 * size, transcendentals=0),
    )(pltpu.with_memory_space_constraint(weight_delta, pltpu.HBM))
    return pl.pallas_call(
        finish_kernel,
        out_shape=jax.ShapeDtypeStruct(resident.shape, resident.dtype),
        in_specs=[pl.BlockSpec(memory_space=pltpu.VMEM)] * 2,
        out_specs=pl.BlockSpec(memory_space=pl.ANY),
        scratch_shapes=[
            pltpu.VMEM(resident.shape, resident.dtype),
            pltpu.SemaphoreType.DMA((-(-feats // CHUNK),)),
        ],
        compiler_params=pltpu.CompilerParams(vmem_limit_bytes=32 * 1024 * 1024),
        cost_estimate=pl.CostEstimate(flops=6 * size, bytes_accessed=4 * size, transcendentals=0),
    )(work, resident)


def solution(mesh):
    placed = (P("inp", "out"), P(("out", "inp"), None))
    return jax.shard_map(
        shards, mesh=mesh, in_specs=placed, out_specs=P(("out", "inp"), None), check_vma=False
    )
```

```python
import functools

import jax
import jax.numpy as jnp
from jax import lax
from jax.experimental import pallas as pl
from jax.experimental.pallas import tpu as pltpu
from jax.sharding import PartitionSpec as P

LANES = 128
SIDE = 4
CORES = 2
CHUNK = 16
FAR_A = ((2, 0), (3, 1))
FAR_B = ((0, 1), (3, 2))
PAIRS = (
    ((2, 2), (2, 3)), ((2, 0), (2, 1)), ((1, 2), (3, 2)), ((1, 1), (3, 1)),
    ((1, 3), (3, 3)), ((1, 0), (3, 0)), ((0, 2), (0, 1)), ((0, 3), (0, 0)),
)
ARRIVALS = (
    (0, 0), (1, 0), (0, 1), (3, 0), (0, 3), (1, 1),
    (3, 3), (1, 3), (3, 1), (2, 0), (0, 2), (2, 3),
)
LAST = (((3, 2),), ((2, 1), (1, 2), (2, 2)))
MESH = pl.DeviceIdType.MESH


def numbers(rows):
    return tuple(sum(row[at] * SIDE**place for place, row in enumerate(rows)) for at in range(len(rows[0])))


def window_of(feats):
    return -(-(CORES * feats + LANES - 1) // LANES) * LANES


def sylvester(order):
    rows = lax.broadcasted_iota(jnp.int32, (order, order), 0)
    cols = lax.broadcasted_iota(jnp.int32, (order, order), 1)
    parity = rows & cols
    for shift in (8, 4, 2, 1):
        parity = parity ^ (parity >> shift)
    return (1 - 2 * (parity & 1)).astype(jnp.float32).astype(jnp.bfloat16)


def selection(order, window, shift):
    rows = lax.broadcasted_iota(jnp.int32, (order, window), 0)
    cols = lax.broadcasted_iota(jnp.int32, (order, window), 1)
    return jnp.where(cols == rows + shift, 1.0, 0.0).astype(jnp.bfloat16)


def butterfly(values):
    values = list(values)
    stride = 1
    while stride < len(values):
        for at in range(len(values)):
            if at & stride == 0:
                first, second = values[at], values[at + stride]
                values[at], values[at + stride] = first + second, first - second
        stride *= 2
    return values


def exchange_kernel(
    update_hbm, work_ref, update, early, sending, middle, relay, received,
    load_sem, early_sems, send_sems, middle_sems, relay_sems, recv_sems,
):
    cols = update.shape[1]
    stacked = received.shape[1]
    feats = stacked // 2
    groups = cols // feats
    window = window_of(feats)
    me = lax.axis_index("inp")
    core = me % CORES
    my_chip = me // CORES
    my_x = my_chip % SIDE
    my_y = my_chip // SIDE
    my_a = my_x + core * (my_y - my_x)
    my_b = my_y + core * (my_x - my_y)

    def chip_at(da, db):
        a, b = (my_a + da) % SIDE, (my_b + db) % SIDE
        x, y = a + core * (b - a), b + core * (a - b)
        return y * SIDE + x

    def device_at(da, db, c):
        return chip_at(da, db) * CORES + c

    def window_at(da, db):
        chip = chip_at(da, db)
        first = jnp.minimum(chip * CORES * feats // LANES, (cols - window) // LANES)
        return pl.ds(pl.multiple_of(first * LANES, LANES), window), chip * CORES * feats - first * LANES

    firsts = [
        pltpu.make_async_copy(update_hbm.at[:, window_at(*PAIRS[0][way])[0]], early.at[way], early_sems.at[way])
        for way in range(2)
    ]
    load = pltpu.make_async_copy(update_hbm, update, load_sem)
    for copy in (*firsts, load):
        copy.start()
    barrier = pltpu.get_barrier_semaphore()
    others = [device_at(da, db, c) for da, db in ((1, 0), (3, 0), (0, 1), (0, 3)) for c in range(CORES)]
    others.append(device_at(0, 0, 1 - core))
    for device in others:
        pl.semaphore_signal(barrier, inc=1, device_id={"inp": device}, device_id_type=MESH)

    def make(da, db, columns=None):
        at, shift = window_at(da, db)
        turned = lax.dot_general(
            selection(CORES * feats, window, shift),
            update[:, at] if columns is None else columns,
            (((1,), (1,)), ((), ())),
            preferred_element_type=jnp.float32,
        )
        for c in range(CORES):
            rows = turned[c * feats : (c + 1) * feats]
            sending[da, db, c] = jnp.concatenate([rows[:, :LANES], rows[:, LANES:]], axis=0).astype(sending.dtype)

    sends = []

    def send(src, dst, sem, device):
        pltpu.make_async_remote_copy(
            src_ref=src, dst_ref=dst, send_sem=send_sems.at[len(sends)], recv_sem=sem,
            device_id={"inp": device}, device_id_type=MESH,
        ).start()
        sends.append(len(src.shape))

    def wait(dst, sem):
        pltpu.make_async_remote_copy(
            src_ref=dst, dst_ref=dst, send_sem=send_sems.at[0], recv_sem=sem,
            device_id={"inp": me}, device_id_type=MESH,
        ).wait_recv()

    def held(da, db):
        return sending.at[da, db] if da == 0 else middle.at[da, db]

    def wait_held(da, db):
        if da != 0:
            wait(middle.at[da, db], middle_sems.at[da, db])

    def to_middle(src, step, da, db):
        send(src, middle.at[da, db], middle_sems.at[da, db], device_at(step, 0, core))

    def to_relay(src, way, slot):
        step = (1, 3)[way % 2]
        da, db = (step, 0) if way < 2 else (0, step)
        send(src, relay.at[way, slot], relay_sems.at[way, slot], device_at(da, db, core))

    def to_ends(blocks):
        for c in range(CORES):
            for src, step, da, db in blocks:
                source = device_at(SIDE - da, db, core)
                send(src.at[c], received.at[source], recv_sems.at[source], device_at(0, step, c))

    def far_a(slot):
        for way in range(2):
            to_relay(sending.at[2, FAR_A[way][slot]], way, slot)

    def near_a(db):
        for da in (1, 3):
            to_middle(sending.at[da, db], da, da, db)

    def far_b(slot):
        for way in (2, 3):
            wait_held(FAR_B[way - 2][slot], 2)
        for way in (2, 3):
            to_relay(held(FAR_B[way - 2][slot], 2), way, slot)

    def near_b(da):
        for db in (1, 3):
            wait_held(da, db)
        to_ends([(held(da, db), db, da, 0) for db in (1, 3)])

    def on_a(slot):
        for way in range(2):
            wait(relay.at[way, slot], relay_sems.at[way, slot])
            to_middle(relay.at[way, slot], (1, 3)[way], 2, FAR_A[way][slot])

    def on_b(slot):
        for way in (2, 3):
            wait(relay.at[way, slot], relay_sems.at[way, slot])
        to_ends([(relay.at[way, slot], step, FAR_B[way - 2][slot], SIDE - step) for way, step in ((2, 1), (3, 3))])

    def home(da):
        wait_held(da, 0)
        block = held(da, 0)
        source = device_at(SIDE - da, 0, core)
        send(block.at[1 - core], received.at[source], recv_sems.at[source], device_at(0, 0, 1 - core))
        received[source] = block[core]

    for way in range(2):
        firsts[way].wait()
    for way in range(2):
        make(*PAIRS[0][way], early[way])
    pl.semaphore_wait(barrier, len(others))
    far_a(0)
    load.wait()

    def second():
        far_a(1)

    def third():
        near_a(2)

    def fourth():
        near_a(1)
        on_a(0)

    def fifth():
        near_a(3)
        on_a(1)

    def sixth():
        near_a(0)

    def seventh():
        far_b(0)

    def make_pair(pair, digits):
        for at in range(2):
            make(digits[2 * at] % SIDE, digits[2 * at + 1] % SIDE)
        for at, action in enumerate((second, third, fourth, fifth, sixth, seventh)):
            pl.when(pair == at)(action)
        return tuple(digit // SIDE for digit in digits)

    lax.fori_loop(0, len(PAIRS) - 1, make_pair, numbers([one + other for one, other in PAIRS[1:]]))
    near_b(0)
    far_b(1)
    near_b(1)
    near_b(3)
    home(0)
    on_b(0)
    near_b(2)
    for da in (1, 3, 2):
        home(da)
    on_b(1)

    matrix = sylvester(2 * LANES)

    def rotate(*chips):
        places = []
        for x, y in chips:
            places.append(((my_x + SIDE - x) % SIDE, (my_y + SIDE - y) % SIDE))
            first = (places[-1][1] * SIDE + places[-1][0]) * CORES
            for c, other in enumerate((y + core, x + 1 - core)):

                @pl.when(other > 0)
                def _(source=first + c):
                    wait(received.at[source], recv_sems.at[source])

        for from_x, from_y in places:
            first = (from_y * SIDE + from_x) * CORES
            pair = jnp.concatenate([received[first], received[first + 1]], axis=1)
            both = jnp.dot(pair, matrix, preferred_element_type=jnp.float32)
            low, high = both[:feats], both[feats:]
            for half, value in enumerate((low + high, low - high)):
                for c in range(CORES):
                    work_ref[from_y, from_x, 2 * c + half] = value[:, c * LANES : (c + 1) * LANES]

    def rotate_pair(_, digits):
        rotate(*((digits[2 * at] % SIDE, digits[2 * at + 1] % SIDE) for at in range(2)))
        return tuple(digit // SIDE for digit in digits)

    pairs = [one + other for one, other in zip(ARRIVALS[::2], ARRIVALS[1::2])]
    lax.fori_loop(0, len(pairs), rotate_pair, numbers(pairs))
    for chips in LAST:
        rotate(*chips)

    for at, dims in enumerate(sends):
        src = received.at[0] if dims == 2 else sending.at[0, 0]
        pltpu.make_async_remote_copy(
            src_ref=src, dst_ref=src, send_sem=send_sems.at[at], recv_sem=send_sems.at[at],
            device_id={"inp": me}, device_id_type=MESH,
        ).wait_send()


def finish_kernel(work_ref, resident, out_hbm, out, out_sems):
    feats, width = out.shape
    factor = 1.0 / jnp.sqrt(jnp.float32(width))
    whole = feats // CHUNK

    def store(chunk, rows):
        return pltpu.make_async_copy(out.at[rows], out_hbm.at[rows], out_sems.at[chunk])

    def finish(rows):
        for at in range(2 * CORES):
            values = butterfly([work_ref[y, x, at, rows, :] for y in range(SIDE) for x in range(SIDE)])
            for chip, value in enumerate(values):
                cols = pl.ds((chip * 2 * CORES + at) * LANES, LANES)
                total = resident[rows, cols].astype(jnp.float32) + value * factor
                out[rows, cols] = total.astype(out.dtype)

    @pl.loop(0, whole)
    def _(chunk):
        rows = pl.ds(pl.multiple_of(chunk * CHUNK, CHUNK), CHUNK)
        finish(rows)
        store(chunk, rows).start()

    rest = pl.ds(whole * CHUNK, feats % CHUNK)
    if feats % CHUNK:
        finish(rest)
        store(whole, rest).start()
        store(whole, rest).wait()

    @pl.loop(0, whole)
    def _(chunk):
        store(chunk, pl.ds(pl.multiple_of(chunk * CHUNK, CHUNK), CHUNK)).wait()


def shards(weight_delta, resident):
    rows, cols = weight_delta.shape
    groups = lax.axis_size("inp")
    feats = cols // groups
    size = rows * cols
    work = pl.pallas_call(
        exchange_kernel,
        out_shape=pltpu.VMEM((SIDE, SIDE, 2 * CORES, feats, LANES), jnp.float32),
        in_specs=[pl.BlockSpec(memory_space=pl.ANY)],
        out_specs=pl.BlockSpec(memory_space=pltpu.VMEM),
        scratch_shapes=[
            pltpu.VMEM((rows, cols), weight_delta.dtype),
            pltpu.VMEM((2, rows, window_of(feats)), weight_delta.dtype),
            pltpu.VMEM((SIDE, SIDE, CORES, 2 * feats, LANES), weight_delta.dtype),
            pltpu.VMEM((SIDE, SIDE, CORES, 2 * feats, LANES), weight_delta.dtype),
            pltpu.VMEM((4, 2, CORES, 2 * feats, LANES), weight_delta.dtype),
            pltpu.VMEM((groups, 2 * feats, LANES), weight_delta.dtype),
            pltpu.SemaphoreType.DMA,
            pltpu.SemaphoreType.DMA((2,)),
            pltpu.SemaphoreType.DMA((64,)),
            pltpu.SemaphoreType.DMA((SIDE, SIDE)),
            pltpu.SemaphoreType.DMA((4, 2)),
            pltpu.SemaphoreType.DMA((groups,)),
        ],
        compiler_params=pltpu.CompilerParams(
            collective_id=0, has_side_effects=True, vmem_limit_bytes=32 * 1024 * 1024
        ),
        cost_estimate=pl.CostEstimate(flops=2 * size * (rows + LANES), bytes_accessed=2 * size, transcendentals=0),
    )(pltpu.with_memory_space_constraint(weight_delta, pltpu.HBM))
    return pl.pallas_call(
        finish_kernel,
        out_shape=jax.ShapeDtypeStruct(resident.shape, resident.dtype),
        in_specs=[pl.BlockSpec(memory_space=pltpu.VMEM)] * 2,
        out_specs=pl.BlockSpec(memory_space=pl.ANY),
        scratch_shapes=[
            pltpu.VMEM(resident.shape, resident.dtype),
            pltpu.SemaphoreType.DMA((-(-feats // CHUNK),)),
        ],
        compiler_params=pltpu.CompilerParams(vmem_limit_bytes=32 * 1024 * 1024),
        cost_estimate=pl.CostEstimate(flops=6 * size, bytes_accessed=4 * size, transcendentals=0),
    )(work, resident)


def solution(mesh):
    placed = (P("inp", "out"), P(("out", "inp"), None))
    return jax.shard_map(
        shards, mesh=mesh, in_specs=placed, out_specs=P(("out", "inp"), None), check_vma=False
    )
```

```python
import functools

import jax
import jax.numpy as jnp
from jax import lax
from jax.experimental import pallas as pl
from jax.experimental.pallas import tpu as pltpu
from jax.sharding import PartitionSpec as P

LANES = 128
SIDE = 4
CORES = 2
CHUNK = 16
FAR_A = ((2, 0), (3, 1))
FAR_B = ((0, 1), (3, 2))
PAIRS = (
    ((2, 2), (2, 3)), ((2, 0), (2, 1)), ((1, 2), (3, 2)), ((1, 1), (3, 1)),
    ((1, 3), (3, 3)), ((1, 0), (3, 0)), ((0, 2), (0, 1)), ((0, 3), (0, 0)),
)
ARRIVALS = (
    (0, 0), (1, 0), (0, 1), (3, 0), (0, 3), (1, 1),
    (2, 0), (0, 2), (2, 3), (3, 2), (2, 1), (1, 2),
)
LAST = (((2, 2),), ((3, 1), (1, 3), (3, 3)))
MESH = pl.DeviceIdType.MESH


def numbers(rows):
    return tuple(sum(row[at] * SIDE**place for place, row in enumerate(rows)) for at in range(len(rows[0])))


def window_of(feats):
    return -(-(CORES * feats + LANES - 1) // LANES) * LANES


def sylvester(order):
    rows = lax.broadcasted_iota(jnp.int32, (order, order), 0)
    cols = lax.broadcasted_iota(jnp.int32, (order, order), 1)
    parity = rows & cols
    for shift in (8, 4, 2, 1):
        parity = parity ^ (parity >> shift)
    return (1 - 2 * (parity & 1)).astype(jnp.float32).astype(jnp.bfloat16)


def selection(order, window, shift):
    rows = lax.broadcasted_iota(jnp.int32, (order, window), 0)
    cols = lax.broadcasted_iota(jnp.int32, (order, window), 1)
    return jnp.where(cols == rows + shift, 1.0, 0.0).astype(jnp.bfloat16)


def butterfly(values):
    values = list(values)
    stride = 1
    while stride < len(values):
        for at in range(len(values)):
            if at & stride == 0:
                first, second = values[at], values[at + stride]
                values[at], values[at + stride] = first + second, first - second
        stride *= 2
    return values


def exchange_kernel(
    update_hbm, work_ref, update, early, sending, middle, relay, received,
    load_sem, early_sems, send_sems, middle_sems, relay_sems, recv_sems,
):
    cols = update.shape[1]
    stacked = received.shape[1]
    feats = stacked // 2
    groups = cols // feats
    window = window_of(feats)
    me = lax.axis_index("inp")
    core = me % CORES
    my_chip = me // CORES
    my_x = my_chip % SIDE
    my_y = my_chip // SIDE
    my_a = my_x + core * (my_y - my_x)
    my_b = my_y + core * (my_x - my_y)

    def chip_at(da, db):
        a, b = (my_a + da) % SIDE, (my_b + db) % SIDE
        x, y = a + core * (b - a), b + core * (a - b)
        return y * SIDE + x

    def device_at(da, db, c):
        return chip_at(da, db) * CORES + c

    def window_at(da, db):
        chip = chip_at(da, db)
        first = jnp.minimum(chip * CORES * feats // LANES, (cols - window) // LANES)
        return pl.ds(pl.multiple_of(first * LANES, LANES), window), chip * CORES * feats - first * LANES

    firsts = [
        pltpu.make_async_copy(update_hbm.at[:, window_at(*PAIRS[0][way])[0]], early.at[way], early_sems.at[way])
        for way in range(2)
    ]
    load = pltpu.make_async_copy(update_hbm, update, load_sem)
    for copy in (*firsts, load):
        copy.start()
    barrier = pltpu.get_barrier_semaphore()
    others = [device_at(da, db, c) for da, db in ((1, 0), (3, 0), (0, 1), (0, 3)) for c in range(CORES)]
    others.append(device_at(0, 0, 1 - core))
    for device in others:
        pl.semaphore_signal(barrier, inc=1, device_id={"inp": device}, device_id_type=MESH)

    def make(da, db, columns=None):
        at, shift = window_at(da, db)
        turned = lax.dot_general(
            selection(CORES * feats, window, shift),
            update[:, at] if columns is None else columns,
            (((1,), (1,)), ((), ())),
            preferred_element_type=jnp.float32,
        )
        for c in range(CORES):
            rows = turned[c * feats : (c + 1) * feats]
            sending[da, db, c] = jnp.concatenate([rows[:, :LANES], rows[:, LANES:]], axis=0).astype(sending.dtype)

    sends = []

    def send(src, dst, sem, device):
        pltpu.make_async_remote_copy(
            src_ref=src, dst_ref=dst, send_sem=send_sems.at[len(sends)], recv_sem=sem,
            device_id={"inp": device}, device_id_type=MESH,
        ).start()
        sends.append(len(src.shape))

    def wait(dst, sem):
        pltpu.make_async_remote_copy(
            src_ref=dst, dst_ref=dst, send_sem=send_sems.at[0], recv_sem=sem,
            device_id={"inp": me}, device_id_type=MESH,
        ).wait_recv()

    def held(da, db):
        return sending.at[da, db] if da == 0 else middle.at[da, db]

    def wait_held(da, db):
        if da != 0:
            wait(middle.at[da, db], middle_sems.at[da, db])

    def to_middle(src, step, da, db):
        send(src, middle.at[da, db], middle_sems.at[da, db], device_at(step, 0, core))

    def to_relay(src, way, slot):
        step = (1, 3)[way % 2]
        da, db = (step, 0) if way < 2 else (0, step)
        send(src, relay.at[way, slot], relay_sems.at[way, slot], device_at(da, db, core))

    def to_ends(blocks):
        for c in range(CORES):
            for src, step, da, db in blocks:
                source = device_at(SIDE - da, db, core)
                send(src.at[c], received.at[source], recv_sems.at[source], device_at(0, step, c))

    def far_a(slot):
        for way in range(2):
            to_relay(sending.at[2, FAR_A[way][slot]], way, slot)

    def near_a(db):
        for da in (1, 3):
            to_middle(sending.at[da, db], da, da, db)

    def far_b(slot):
        for way in (2, 3):
            wait_held(FAR_B[way - 2][slot], 2)
        for way in (2, 3):
            to_relay(held(FAR_B[way - 2][slot], 2), way, slot)

    def near_b(da):
        for db in (1, 3):
            wait_held(da, db)
        to_ends([(held(da, db), db, da, 0) for db in (1, 3)])

    def on_a(slot):
        for way in range(2):
            wait(relay.at[way, slot], relay_sems.at[way, slot])
            to_middle(relay.at[way, slot], (1, 3)[way], 2, FAR_A[way][slot])

    def on_b(slot):
        for way in (2, 3):
            wait(relay.at[way, slot], relay_sems.at[way, slot])
        to_ends([(relay.at[way, slot], step, FAR_B[way - 2][slot], SIDE - step) for way, step in ((2, 1), (3, 3))])

    def home(da):
        wait_held(da, 0)
        block = held(da, 0)
        source = device_at(SIDE - da, 0, core)
        send(block.at[1 - core], received.at[source], recv_sems.at[source], device_at(0, 0, 1 - core))
        received[source] = block[core]

    for way in range(2):
        firsts[way].wait()
    for way in range(2):
        make(*PAIRS[0][way], early[way])
    pl.semaphore_wait(barrier, len(others))
    far_a(0)
    load.wait()

    def second():
        far_a(1)

    def third():
        near_a(2)

    def fourth():
        near_a(1)
        on_a(0)

    def fifth():
        near_a(3)
        on_a(1)

    def sixth():
        near_a(0)

    def seventh():
        far_b(0)

    def make_pair(pair, digits):
        for at in range(2):
            make(digits[2 * at] % SIDE, digits[2 * at + 1] % SIDE)
        for at, action in enumerate((second, third, fourth, fifth, sixth, seventh)):
            pl.when(pair == at)(action)
        return tuple(digit // SIDE for digit in digits)

    lax.fori_loop(0, len(PAIRS) - 1, make_pair, numbers([one + other for one, other in PAIRS[1:]]))
    near_b(0)
    far_b(1)
    near_b(1)
    near_b(2)
    on_b(0)
    on_b(1)
    near_b(3)
    for da in (0, 1, 3, 2):
        home(da)

    matrix = sylvester(2 * LANES)

    def rotate(*chips):
        places = []
        for x, y in chips:
            places.append(((my_x + SIDE - x) % SIDE, (my_y + SIDE - y) % SIDE))
            first = (places[-1][1] * SIDE + places[-1][0]) * CORES
            for c, other in enumerate((y + core, x + 1 - core)):

                @pl.when(other > 0)
                def _(source=first + c):
                    wait(received.at[source], recv_sems.at[source])

        for from_x, from_y in places:
            first = (from_y * SIDE + from_x) * CORES
            pair = jnp.concatenate([received[first], received[first + 1]], axis=1)
            both = jnp.dot(pair, matrix, preferred_element_type=jnp.float32)
            low, high = both[:feats], both[feats:]
            for half, value in enumerate((low + high, low - high)):
                for c in range(CORES):
                    work_ref[from_y, from_x, 2 * c + half] = value[:, c * LANES : (c + 1) * LANES]

    def rotate_pair(_, digits):
        rotate(*((digits[2 * at] % SIDE, digits[2 * at + 1] % SIDE) for at in range(2)))
        return tuple(digit // SIDE for digit in digits)

    pairs = [one + other for one, other in zip(ARRIVALS[::2], ARRIVALS[1::2])]
    lax.fori_loop(0, len(pairs), rotate_pair, numbers(pairs))
    for chips in LAST:
        rotate(*chips)

    for at, dims in enumerate(sends):
        src = received.at[0] if dims == 2 else sending.at[0, 0]
        pltpu.make_async_remote_copy(
            src_ref=src, dst_ref=src, send_sem=send_sems.at[at], recv_sem=send_sems.at[at],
            device_id={"inp": me}, device_id_type=MESH,
        ).wait_send()


def finish_kernel(work_ref, resident, out_hbm, out, out_sems):
    feats, width = out.shape
    factor = 1.0 / jnp.sqrt(jnp.float32(width))
    whole = feats // CHUNK

    def store(chunk, rows):
        return pltpu.make_async_copy(out.at[rows], out_hbm.at[rows], out_sems.at[chunk])

    def finish(rows):
        for at in range(2 * CORES):
            values = butterfly([work_ref[y, x, at, rows, :] for y in range(SIDE) for x in range(SIDE)])
            for chip, value in enumerate(values):
                cols = pl.ds((chip * 2 * CORES + at) * LANES, LANES)
                total = resident[rows, cols].astype(jnp.float32) + value * factor
                out[rows, cols] = total.astype(out.dtype)

    @pl.loop(0, whole)
    def _(chunk):
        rows = pl.ds(pl.multiple_of(chunk * CHUNK, CHUNK), CHUNK)
        finish(rows)
        store(chunk, rows).start()

    rest = pl.ds(whole * CHUNK, feats % CHUNK)
    if feats % CHUNK:
        finish(rest)
        store(whole, rest).start()
        store(whole, rest).wait()

    @pl.loop(0, whole)
    def _(chunk):
        store(chunk, pl.ds(pl.multiple_of(chunk * CHUNK, CHUNK), CHUNK)).wait()


def shards(weight_delta, resident):
    rows, cols = weight_delta.shape
    groups = lax.axis_size("inp")
    feats = cols // groups
    size = rows * cols
    work = pl.pallas_call(
        exchange_kernel,
        out_shape=pltpu.VMEM((SIDE, SIDE, 2 * CORES, feats, LANES), jnp.float32),
        in_specs=[pl.BlockSpec(memory_space=pl.ANY)],
        out_specs=pl.BlockSpec(memory_space=pltpu.VMEM),
        scratch_shapes=[
            pltpu.VMEM((rows, cols), weight_delta.dtype),
            pltpu.VMEM((2, rows, window_of(feats)), weight_delta.dtype),
            pltpu.VMEM((SIDE, SIDE, CORES, 2 * feats, LANES), weight_delta.dtype),
            pltpu.VMEM((SIDE, SIDE, CORES, 2 * feats, LANES), weight_delta.dtype),
            pltpu.VMEM((4, 2, CORES, 2 * feats, LANES), weight_delta.dtype),
            pltpu.VMEM((groups, 2 * feats, LANES), weight_delta.dtype),
            pltpu.SemaphoreType.DMA,
            pltpu.SemaphoreType.DMA((2,)),
            pltpu.SemaphoreType.DMA((64,)),
            pltpu.SemaphoreType.DMA((SIDE, SIDE)),
            pltpu.SemaphoreType.DMA((4, 2)),
            pltpu.SemaphoreType.DMA((groups,)),
        ],
        compiler_params=pltpu.CompilerParams(
            collective_id=0, has_side_effects=True, vmem_limit_bytes=32 * 1024 * 1024
        ),
        cost_estimate=pl.CostEstimate(flops=2 * size * (rows + LANES), bytes_accessed=2 * size, transcendentals=0),
    )(pltpu.with_memory_space_constraint(weight_delta, pltpu.HBM))
    return pl.pallas_call(
        finish_kernel,
        out_shape=jax.ShapeDtypeStruct(resident.shape, resident.dtype),
        in_specs=[pl.BlockSpec(memory_space=pltpu.VMEM)] * 2,
        out_specs=pl.BlockSpec(memory_space=pl.ANY),
        scratch_shapes=[
            pltpu.VMEM(resident.shape, resident.dtype),
            pltpu.SemaphoreType.DMA((-(-feats // CHUNK),)),
        ],
        compiler_params=pltpu.CompilerParams(vmem_limit_bytes=32 * 1024 * 1024),
        cost_estimate=pl.CostEstimate(flops=6 * size, bytes_accessed=4 * size, transcendentals=0),
    )(work, resident)


def solution(mesh):
    placed = (P("inp", "out"), P(("out", "inp"), None))
    return jax.shard_map(
        shards, mesh=mesh, in_specs=placed, out_specs=P(("out", "inp"), None), check_vma=False
    )
```

```python
import functools

import jax
import jax.numpy as jnp
from jax import lax
from jax.experimental import pallas as pl
from jax.experimental.pallas import tpu as pltpu
from jax.sharding import PartitionSpec as P

LANES = 128
SIDE = 4
CORES = 2
CHUNK = 16
FAR_A = ((2, 0), (3, 1))
FAR_B = ((0, 1), (3, 2))
PAIRS = (
    ((2, 2), (2, 3)), ((2, 0), (2, 1)), ((1, 2), (3, 2)), ((1, 1), (3, 1)),
    ((1, 3), (3, 3)), ((1, 0), (3, 0)), ((0, 2), (0, 1)), ((0, 3), (0, 0)),
)
ARRIVALS = (
    (0, 0), (1, 0), (0, 1), (3, 0), (0, 3), (1, 1),
    (3, 3), (1, 3), (3, 1), (2, 0), (0, 2), (2, 3),
)
LAST = (((3, 2),), ((2, 1), (1, 2), (2, 2)))
MESH = pl.DeviceIdType.MESH


def numbers(rows):
    return tuple(sum(row[at] * SIDE**place for place, row in enumerate(rows)) for at in range(len(rows[0])))


def window_of(feats):
    return -(-(CORES * feats + LANES - 1) // LANES) * LANES


def sylvester(order):
    rows = lax.broadcasted_iota(jnp.int32, (order, order), 0)
    cols = lax.broadcasted_iota(jnp.int32, (order, order), 1)
    parity = rows & cols
    for shift in (8, 4, 2, 1):
        parity = parity ^ (parity >> shift)
    return (1 - 2 * (parity & 1)).astype(jnp.float32).astype(jnp.bfloat16)


def identity(order):
    rows = lax.broadcasted_iota(jnp.int32, (order, order), 0)
    cols = lax.broadcasted_iota(jnp.int32, (order, order), 1)
    return jnp.where(rows == cols, 1.0, 0.0).astype(jnp.bfloat16)


def butterfly(values):
    values = list(values)
    stride = 1
    while stride < len(values):
        for at in range(len(values)):
            if at & stride == 0:
                first, second = values[at], values[at + stride]
                values[at], values[at + stride] = first + second, first - second
        stride *= 2
    return values


def exchange_kernel(
    update_hbm, work_ref, update, early, eye, sending, middle, relay, received,
    load_sem, early_sems, send_sems, middle_sems, relay_sems, recv_sems,
):
    cols = update.shape[1]
    stacked = received.shape[1]
    feats = stacked // 2
    groups = cols // feats
    window = window_of(feats)
    me = lax.axis_index("inp")
    core = me % CORES
    my_chip = me // CORES
    my_x = my_chip % SIDE
    my_y = my_chip // SIDE
    my_a = my_x + core * (my_y - my_x)
    my_b = my_y + core * (my_x - my_y)

    def chip_at(da, db):
        a, b = (my_a + da) % SIDE, (my_b + db) % SIDE
        x, y = a + core * (b - a), b + core * (a - b)
        return y * SIDE + x

    def device_at(da, db, c):
        return chip_at(da, db) * CORES + c

    def window_at(da, db):
        chip = chip_at(da, db)
        first = jnp.minimum(chip * CORES * feats // LANES, (cols - window) // LANES)
        return pl.ds(pl.multiple_of(first * LANES, LANES), window), chip * CORES * feats - first * LANES

    firsts = [
        pltpu.make_async_copy(update_hbm.at[:, window_at(*PAIRS[0][way])[0]], early.at[way], early_sems.at[way])
        for way in range(2)
    ]
    load = pltpu.make_async_copy(update_hbm, update, load_sem)
    for copy in (*firsts, load):
        copy.start()
    barrier = pltpu.get_barrier_semaphore()
    others = [device_at(da, db, c) for da, db in ((1, 0), (3, 0), (0, 1), (0, 3)) for c in range(CORES)]
    others.append(device_at(0, 0, 1 - core))
    for device in others:
        pl.semaphore_signal(barrier, inc=1, device_id={"inp": device}, device_id_type=MESH)

    def make(da, db, columns=None):
        at, shift = window_at(da, db)
        turned = lax.dot_general(
            eye[pl.ds(pl.multiple_of(shift, 16), CORES * feats), :],
            update[:, at] if columns is None else columns,
            (((1,), (1,)), ((), ())),
            preferred_element_type=jnp.float32,
        )
        for c in range(CORES):
            rows = turned[c * feats : (c + 1) * feats]
            sending[da, db, c] = jnp.concatenate([rows[:, :LANES], rows[:, LANES:]], axis=0).astype(sending.dtype)

    sends = []

    def send(src, dst, sem, device):
        pltpu.make_async_remote_copy(
            src_ref=src, dst_ref=dst, send_sem=send_sems.at[len(sends)], recv_sem=sem,
            device_id={"inp": device}, device_id_type=MESH,
        ).start()
        sends.append(len(src.shape))

    def wait(dst, sem):
        pltpu.make_async_remote_copy(
            src_ref=dst, dst_ref=dst, send_sem=send_sems.at[0], recv_sem=sem,
            device_id={"inp": me}, device_id_type=MESH,
        ).wait_recv()

    def held(da, db):
        return sending.at[da, db] if da == 0 else middle.at[da, db]

    def wait_held(da, db):
        if da != 0:
            wait(middle.at[da, db], middle_sems.at[da, db])

    def to_middle(src, step, da, db):
        send(src, middle.at[da, db], middle_sems.at[da, db], device_at(step, 0, core))

    def to_relay(src, way, slot):
        step = (1, 3)[way % 2]
        da, db = (step, 0) if way < 2 else (0, step)
        send(src, relay.at[way, slot], relay_sems.at[way, slot], device_at(da, db, core))

    def to_ends(blocks):
        for c in range(CORES):
            for src, step, da, db in blocks:
                source = device_at(SIDE - da, db, core)
                send(src.at[c], received.at[source], recv_sems.at[source], device_at(0, step, c))

    def far_a(slot):
        for way in range(2):
            to_relay(sending.at[2, FAR_A[way][slot]], way, slot)

    def near_a(db):
        for da in (1, 3):
            to_middle(sending.at[da, db], da, da, db)

    def far_b(slot):
        for way in (2, 3):
            wait_held(FAR_B[way - 2][slot], 2)
        for way in (2, 3):
            to_relay(held(FAR_B[way - 2][slot], 2), way, slot)

    def near_b(da):
        for db in (1, 3):
            wait_held(da, db)
        to_ends([(held(da, db), db, da, 0) for db in (1, 3)])

    def on_a(slot):
        for way in range(2):
            wait(relay.at[way, slot], relay_sems.at[way, slot])
            to_middle(relay.at[way, slot], (1, 3)[way], 2, FAR_A[way][slot])

    def on_b(slot):
        for way in (2, 3):
            wait(relay.at[way, slot], relay_sems.at[way, slot])
        to_ends([(relay.at[way, slot], step, FAR_B[way - 2][slot], SIDE - step) for way, step in ((2, 1), (3, 3))])

    def home(da):
        wait_held(da, 0)
        block = held(da, 0)
        source = device_at(SIDE - da, 0, core)
        send(block.at[1 - core], received.at[source], recv_sems.at[source], device_at(0, 0, 1 - core))
        received[source] = block[core]

    eye[...] = identity(window)
    for way in range(2):
        firsts[way].wait()
    for way in range(2):
        make(*PAIRS[0][way], early[way])
    pl.semaphore_wait(barrier, len(others))
    far_a(0)
    load.wait()

    def second():
        far_a(1)

    def third():
        near_a(2)

    def fourth():
        near_a(1)
        on_a(0)

    def fifth():
        near_a(3)
        on_a(1)

    def sixth():
        near_a(0)

    def seventh():
        far_b(0)

    def make_pair(pair, digits):
        for at in range(2):
            make(digits[2 * at] % SIDE, digits[2 * at + 1] % SIDE)
        for at, action in enumerate((second, third, fourth, fifth, sixth, seventh)):
            pl.when(pair == at)(action)
        return tuple(digit // SIDE for digit in digits)

    lax.fori_loop(0, len(PAIRS) - 1, make_pair, numbers([one + other for one, other in PAIRS[1:]]))
    near_b(0)
    far_b(1)
    near_b(1)
    near_b(3)
    home(0)
    on_b(0)
    near_b(2)
    for da in (1, 3, 2):
        home(da)
    on_b(1)

    matrix = sylvester(2 * LANES)
    factor = 1.0 / jnp.sqrt(jnp.float32(groups * 2 * LANES))

    def rotate(*chips):
        places = []
        for x, y in chips:
            places.append(((my_x + SIDE - x) % SIDE, (my_y + SIDE - y) % SIDE))
            first = (places[-1][1] * SIDE + places[-1][0]) * CORES
            for c, other in enumerate((y + core, x + 1 - core)):

                @pl.when(other > 0)
                def _(source=first + c):
                    wait(received.at[source], recv_sems.at[source])

        for from_x, from_y in places:
            first = (from_y * SIDE + from_x) * CORES
            pair = jnp.concatenate([received[first], received[first + 1]], axis=1)
            both = jnp.dot(pair, matrix, preferred_element_type=jnp.float32)
            low, high = both[:feats], both[feats:]
            for half, value in enumerate((low + high, low - high)):
                for c in range(CORES):
                    work_ref[from_y, from_x, 2 * c + half] = value[:, c * LANES : (c + 1) * LANES] * factor

    def rotate_pair(_, digits):
        rotate(*((digits[2 * at] % SIDE, digits[2 * at + 1] % SIDE) for at in range(2)))
        return tuple(digit // SIDE for digit in digits)

    pairs = [one + other for one, other in zip(ARRIVALS[::2], ARRIVALS[1::2])]
    lax.fori_loop(0, len(pairs), rotate_pair, numbers(pairs))
    for chips in LAST:
        rotate(*chips)

    for at, dims in enumerate(sends):
        src = received.at[0] if dims == 2 else sending.at[0, 0]
        pltpu.make_async_remote_copy(
            src_ref=src, dst_ref=src, send_sem=send_sems.at[at], recv_sem=send_sems.at[at],
            device_id={"inp": me}, device_id_type=MESH,
        ).wait_send()


def finish_kernel(work_ref, resident, out_hbm, out, out_sems):
    feats, width = out.shape
    whole = feats // CHUNK

    def store(chunk, rows):
        return pltpu.make_async_copy(out.at[rows], out_hbm.at[rows], out_sems.at[chunk])

    def finish(rows):
        for at in range(2 * CORES):
            values = butterfly([work_ref[y, x, at, rows, :] for y in range(SIDE) for x in range(SIDE)])
            for chip, value in enumerate(values):
                cols = pl.ds((chip * 2 * CORES + at) * LANES, LANES)
                total = resident[rows, cols].astype(jnp.float32) + value
                out[rows, cols] = total.astype(out.dtype)

    @pl.loop(0, whole)
    def _(chunk):
        rows = pl.ds(pl.multiple_of(chunk * CHUNK, CHUNK), CHUNK)
        finish(rows)
        store(chunk, rows).start()

    rest = pl.ds(whole * CHUNK, feats % CHUNK)
    if feats % CHUNK:
        finish(rest)
        store(whole, rest).start()
        store(whole, rest).wait()

    @pl.loop(0, whole)
    def _(chunk):
        store(chunk, pl.ds(pl.multiple_of(chunk * CHUNK, CHUNK), CHUNK)).wait()


def shards(weight_delta, resident):
    rows, cols = weight_delta.shape
    groups = lax.axis_size("inp")
    feats = cols // groups
    size = rows * cols
    work = pl.pallas_call(
        exchange_kernel,
        out_shape=pltpu.VMEM((SIDE, SIDE, 2 * CORES, feats, LANES), jnp.float32),
        in_specs=[pl.BlockSpec(memory_space=pl.ANY)],
        out_specs=pl.BlockSpec(memory_space=pltpu.VMEM),
        scratch_shapes=[
            pltpu.VMEM((rows, cols), weight_delta.dtype),
            pltpu.VMEM((2, rows, window_of(feats)), weight_delta.dtype),
            pltpu.VMEM((window_of(feats), window_of(feats)), weight_delta.dtype),
            pltpu.VMEM((SIDE, SIDE, CORES, 2 * feats, LANES), weight_delta.dtype),
            pltpu.VMEM((SIDE, SIDE, CORES, 2 * feats, LANES), weight_delta.dtype),
            pltpu.VMEM((4, 2, CORES, 2 * feats, LANES), weight_delta.dtype),
            pltpu.VMEM((groups, 2 * feats, LANES), weight_delta.dtype),
            pltpu.SemaphoreType.DMA,
            pltpu.SemaphoreType.DMA((2,)),
            pltpu.SemaphoreType.DMA((64,)),
            pltpu.SemaphoreType.DMA((SIDE, SIDE)),
            pltpu.SemaphoreType.DMA((4, 2)),
            pltpu.SemaphoreType.DMA((groups,)),
        ],
        compiler_params=pltpu.CompilerParams(
            collective_id=0, has_side_effects=True, vmem_limit_bytes=32 * 1024 * 1024
        ),
        cost_estimate=pl.CostEstimate(flops=2 * size * (rows + LANES), bytes_accessed=2 * size, transcendentals=0),
    )(pltpu.with_memory_space_constraint(weight_delta, pltpu.HBM))
    return pl.pallas_call(
        finish_kernel,
        out_shape=jax.ShapeDtypeStruct(resident.shape, resident.dtype),
        in_specs=[pl.BlockSpec(memory_space=pltpu.VMEM)] * 2,
        out_specs=pl.BlockSpec(memory_space=pl.ANY),
        scratch_shapes=[
            pltpu.VMEM(resident.shape, resident.dtype),
            pltpu.SemaphoreType.DMA((-(-feats // CHUNK),)),
        ],
        compiler_params=pltpu.CompilerParams(vmem_limit_bytes=32 * 1024 * 1024),
        cost_estimate=pl.CostEstimate(flops=6 * size, bytes_accessed=4 * size, transcendentals=0),
    )(work, resident)


def solution(mesh):
    placed = (P("inp", "out"), P(("out", "inp"), None))
    return jax.shard_map(
        shards, mesh=mesh, in_specs=placed, out_specs=P(("out", "inp"), None), check_vma=False
    )
```

```python
import functools

import jax
import jax.numpy as jnp
from jax import lax
from jax.experimental import pallas as pl
from jax.experimental.pallas import tpu as pltpu
from jax.sharding import PartitionSpec as P

LANES = 128
SIDE = 4
CORES = 2
CHUNK = 16
FAR_A = ((2, 0), (3, 1))
FAR_B = ((0, 1), (3, 2))
PAIRS = (
    ((2, 2), (2, 3)), ((2, 0), (2, 1)), ((1, 2), (3, 2)), ((1, 1), (3, 1)),
    ((1, 3), (3, 3)), ((1, 0), (3, 0)), ((0, 2), (0, 1)), ((0, 3), (0, 0)),
)
ARRIVALS = (
    (0, 0), (1, 0), (0, 1), (3, 0), (0, 3), (1, 1),
    (3, 3), (1, 3), (3, 1), (2, 0), (0, 2), (2, 3),
)
LAST = (((3, 2),), ((2, 1), (1, 2), (2, 2)))
ALONG_A, ALONG_B, HOME = range(3)
MESH = pl.DeviceIdType.MESH


def numbers(rows):
    return tuple(sum(row[at] * SIDE**place for place, row in enumerate(rows)) for at in range(len(rows[0])))


def window_of(feats):
    return -(-(CORES * feats + LANES - 1) // LANES) * LANES


def sylvester(order):
    rows = lax.broadcasted_iota(jnp.int32, (order, order), 0)
    cols = lax.broadcasted_iota(jnp.int32, (order, order), 1)
    parity = rows & cols
    for shift in (8, 4, 2, 1):
        parity = parity ^ (parity >> shift)
    return (1 - 2 * (parity & 1)).astype(jnp.float32).astype(jnp.bfloat16)


def identity(order):
    rows = lax.broadcasted_iota(jnp.int32, (order, order), 0)
    cols = lax.broadcasted_iota(jnp.int32, (order, order), 1)
    return jnp.where(rows == cols, 1.0, 0.0).astype(jnp.bfloat16)


def butterfly(values):
    values = list(values)
    stride = 1
    while stride < len(values):
        for at in range(len(values)):
            if at & stride == 0:
                first, second = values[at], values[at + stride]
                values[at], values[at + stride] = first + second, first - second
        stride *= 2
    return values


def exchange_kernel(
    update_hbm, work_ref, update, early, eye, sending, middle, relay, received,
    load_sem, early_sems, send_sems, middle_sems, relay_sems, recv_sems,
):
    cols = update.shape[1]
    stacked = received.shape[1]
    feats = stacked // 2
    groups = cols // feats
    window = window_of(feats)
    me = lax.axis_index("inp")
    core = me % CORES
    my_chip = me // CORES
    my_x = my_chip % SIDE
    my_y = my_chip // SIDE
    my_a = my_x + core * (my_y - my_x)
    my_b = my_y + core * (my_x - my_y)

    def chip_at(da, db):
        a, b = (my_a + da) % SIDE, (my_b + db) % SIDE
        x, y = a + core * (b - a), b + core * (a - b)
        return y * SIDE + x

    def device_at(da, db, c):
        return chip_at(da, db) * CORES + c

    def window_at(da, db):
        chip = chip_at(da, db)
        first = jnp.minimum(chip * CORES * feats // LANES, (cols - window) // LANES)
        return pl.ds(pl.multiple_of(first * LANES, LANES), window), chip * CORES * feats - first * LANES

    firsts = [
        pltpu.make_async_copy(update_hbm.at[:, window_at(*PAIRS[0][way])[0]], early.at[way], early_sems.at[way])
        for way in range(2)
    ]
    load = pltpu.make_async_copy(update_hbm, update, load_sem)
    for copy in (*firsts, load):
        copy.start()
    barrier = pltpu.get_barrier_semaphore()
    others = [device_at(da, db, c) for da, db in ((1, 0), (3, 0), (0, 1), (0, 3)) for c in range(CORES)]
    others.append(device_at(0, 0, 1 - core))
    for device in others:
        pl.semaphore_signal(barrier, inc=1, device_id={"inp": device}, device_id_type=MESH)

    def make(da, db, columns=None):
        at, shift = window_at(da, db)
        turned = lax.dot_general(
            eye[pl.ds(pl.multiple_of(shift, 16), CORES * feats), :],
            update[:, at] if columns is None else columns,
            (((1,), (1,)), ((), ())),
            preferred_element_type=jnp.float32,
        )
        for c in range(CORES):
            rows = turned[c * feats : (c + 1) * feats]
            sending[da, db, c] = jnp.concatenate([rows[:, :LANES], rows[:, LANES:]], axis=0).astype(sending.dtype)

    def send(src, dst, kind, sem, device):
        pltpu.make_async_remote_copy(
            src_ref=src, dst_ref=dst, send_sem=send_sems.at[kind], recv_sem=sem,
            device_id={"inp": device}, device_id_type=MESH,
        ).start()

    def wait(dst, sem):
        pltpu.make_async_remote_copy(
            src_ref=dst, dst_ref=dst, send_sem=send_sems.at[0], recv_sem=sem,
            device_id={"inp": me}, device_id_type=MESH,
        ).wait_recv()

    def held(da, db):
        return sending.at[da, db] if da == 0 else middle.at[da, db]

    def wait_held(da, db):
        if da != 0:
            wait(middle.at[da, db], middle_sems.at[da, db])

    def to_middle(src, step, da, db):
        send(src, middle.at[da, db], ALONG_A, middle_sems.at[da, db], device_at(step, 0, core))

    def to_relay(src, way, slot):
        step = (1, 3)[way % 2]
        da, db = (step, 0) if way < 2 else (0, step)
        send(src, relay.at[way, slot], way // 2, relay_sems.at[way, slot], device_at(da, db, core))

    def to_ends(blocks):
        for c in range(CORES):
            for src, step, da, db in blocks:
                source = device_at(SIDE - da, db, core)
                send(src.at[c], received.at[source], ALONG_B, recv_sems.at[source], device_at(0, step, c))

    def far_a(slot):
        for way in range(2):
            to_relay(sending.at[2, FAR_A[way][slot]], way, slot)

    def near_a(db):
        for da in (1, 3):
            to_middle(sending.at[da, db], da, da, db)

    def far_b(slot):
        for way in (2, 3):
            wait_held(FAR_B[way - 2][slot], 2)
        for way in (2, 3):
            to_relay(held(FAR_B[way - 2][slot], 2), way, slot)

    def near_b(da):
        for db in (1, 3):
            wait_held(da, db)
        to_ends([(held(da, db), db, da, 0) for db in (1, 3)])

    def on_a(slot):
        for way in range(2):
            wait(relay.at[way, slot], relay_sems.at[way, slot])
            to_middle(relay.at[way, slot], (1, 3)[way], 2, FAR_A[way][slot])

    def on_b(slot):
        for way in (2, 3):
            wait(relay.at[way, slot], relay_sems.at[way, slot])
        to_ends([(relay.at[way, slot], step, FAR_B[way - 2][slot], SIDE - step) for way, step in ((2, 1), (3, 3))])

    def home(da):
        wait_held(da, 0)
        block = held(da, 0)
        source = device_at(SIDE - da, 0, core)
        send(block.at[1 - core], received.at[source], HOME, recv_sems.at[source], device_at(0, 0, 1 - core))
        received[source] = block[core]

    eye[...] = identity(window)
    for way in range(2):
        firsts[way].wait()
    for way in range(2):
        make(*PAIRS[0][way], early[way])
    pl.semaphore_wait(barrier, len(others))
    far_a(0)
    load.wait()

    def second():
        far_a(1)

    def third():
        near_a(2)

    def fourth():
        near_a(1)
        on_a(0)

    def fifth():
        near_a(3)
        on_a(1)

    def sixth():
        near_a(0)

    def seventh():
        far_b(0)

    def make_pair(pair, digits):
        for at in range(2):
            make(digits[2 * at] % SIDE, digits[2 * at + 1] % SIDE)
        for at, action in enumerate((second, third, fourth, fifth, sixth, seventh)):
            pl.when(pair == at)(action)
        return tuple(digit // SIDE for digit in digits)

    lax.fori_loop(0, len(PAIRS) - 1, make_pair, numbers([one + other for one, other in PAIRS[1:]]))
    near_b(0)
    far_b(1)
    near_b(1)
    near_b(3)
    home(0)
    on_b(0)
    near_b(2)
    for da in (1, 3, 2):
        home(da)
    on_b(1)

    matrix = sylvester(2 * LANES)
    factor = 1.0 / jnp.sqrt(jnp.float32(groups * 2 * LANES))

    def rotate(*chips):
        places = []
        for x, y in chips:
            places.append(((my_x + SIDE - x) % SIDE, (my_y + SIDE - y) % SIDE))
            first = (places[-1][1] * SIDE + places[-1][0]) * CORES
            for c, other in enumerate((y + core, x + 1 - core)):

                @pl.when(other > 0)
                def _(source=first + c):
                    wait(received.at[source], recv_sems.at[source])

        for from_x, from_y in places:
            first = (from_y * SIDE + from_x) * CORES
            pair = jnp.concatenate([received[first], received[first + 1]], axis=1)
            both = jnp.dot(pair, matrix, preferred_element_type=jnp.float32)
            low, high = both[:feats], both[feats:]
            for half, value in enumerate((low + high, low - high)):
                for c in range(CORES):
                    work_ref[from_y, from_x, 2 * c + half] = value[:, c * LANES : (c + 1) * LANES] * factor

    def rotate_pair(_, digits):
        rotate(*((digits[2 * at] % SIDE, digits[2 * at + 1] % SIDE) for at in range(2)))
        return tuple(digit // SIDE for digit in digits)

    pairs = [one + other for one, other in zip(ARRIVALS[::2], ARRIVALS[1::2])]
    lax.fori_loop(0, len(pairs), rotate_pair, numbers(pairs))
    for chips in LAST:
        rotate(*chips)

    for kind, sent in ((ALONG_A, sending), (ALONG_B, sending), (HOME, received.at[pl.ds(0, SIDE)])):
        pltpu.make_async_remote_copy(
            src_ref=sent, dst_ref=sent, send_sem=send_sems.at[kind], recv_sem=send_sems.at[kind],
            device_id={"inp": me}, device_id_type=MESH,
        ).wait_send()


def finish_kernel(work_ref, resident, out_hbm, out, out_sems):
    feats, width = out.shape
    whole = feats // CHUNK

    def store(chunk, rows):
        return pltpu.make_async_copy(out.at[rows], out_hbm.at[rows], out_sems.at[chunk])

    def finish(rows):
        for at in range(2 * CORES):
            values = butterfly([work_ref[y, x, at, rows, :] for y in range(SIDE) for x in range(SIDE)])
            for chip, value in enumerate(values):
                cols = pl.ds((chip * 2 * CORES + at) * LANES, LANES)
                total = resident[rows, cols].astype(jnp.float32) + value
                out[rows, cols] = total.astype(out.dtype)

    @pl.loop(0, whole)
    def _(chunk):
        rows = pl.ds(pl.multiple_of(chunk * CHUNK, CHUNK), CHUNK)
        finish(rows)
        store(chunk, rows).start()

    rest = pl.ds(whole * CHUNK, feats % CHUNK)
    if feats % CHUNK:
        finish(rest)
        store(whole, rest).start()
        store(whole, rest).wait()

    @pl.loop(0, whole)
    def _(chunk):
        store(chunk, pl.ds(pl.multiple_of(chunk * CHUNK, CHUNK), CHUNK)).wait()


def shards(weight_delta, resident):
    rows, cols = weight_delta.shape
    groups = lax.axis_size("inp")
    feats = cols // groups
    size = rows * cols
    work = pl.pallas_call(
        exchange_kernel,
        out_shape=pltpu.VMEM((SIDE, SIDE, 2 * CORES, feats, LANES), jnp.float32),
        in_specs=[pl.BlockSpec(memory_space=pl.ANY)],
        out_specs=pl.BlockSpec(memory_space=pltpu.VMEM),
        scratch_shapes=[
            pltpu.VMEM((rows, cols), weight_delta.dtype),
            pltpu.VMEM((2, rows, window_of(feats)), weight_delta.dtype),
            pltpu.VMEM((window_of(feats), window_of(feats)), weight_delta.dtype),
            pltpu.VMEM((SIDE, SIDE, CORES, 2 * feats, LANES), weight_delta.dtype),
            pltpu.VMEM((SIDE, SIDE, CORES, 2 * feats, LANES), weight_delta.dtype),
            pltpu.VMEM((4, 2, CORES, 2 * feats, LANES), weight_delta.dtype),
            pltpu.VMEM((groups, 2 * feats, LANES), weight_delta.dtype),
            pltpu.SemaphoreType.DMA,
            pltpu.SemaphoreType.DMA((2,)),
            pltpu.SemaphoreType.DMA((3,)),
            pltpu.SemaphoreType.DMA((SIDE, SIDE)),
            pltpu.SemaphoreType.DMA((4, 2)),
            pltpu.SemaphoreType.DMA((groups,)),
        ],
        compiler_params=pltpu.CompilerParams(
            collective_id=0, has_side_effects=True, vmem_limit_bytes=32 * 1024 * 1024
        ),
        cost_estimate=pl.CostEstimate(flops=2 * size * (rows + LANES), bytes_accessed=2 * size, transcendentals=0),
    )(pltpu.with_memory_space_constraint(weight_delta, pltpu.HBM))
    return pl.pallas_call(
        finish_kernel,
        out_shape=jax.ShapeDtypeStruct(resident.shape, resident.dtype),
        in_specs=[pl.BlockSpec(memory_space=pltpu.VMEM)] * 2,
        out_specs=pl.BlockSpec(memory_space=pl.ANY),
        scratch_shapes=[
            pltpu.VMEM(resident.shape, resident.dtype),
            pltpu.SemaphoreType.DMA((-(-feats // CHUNK),)),
        ],
        compiler_params=pltpu.CompilerParams(vmem_limit_bytes=32 * 1024 * 1024),
        cost_estimate=pl.CostEstimate(flops=6 * size, bytes_accessed=4 * size, transcendentals=0),
    )(work, resident)


def solution(mesh):
    placed = (P("inp", "out"), P(("out", "inp"), None))
    return jax.shard_map(
        shards, mesh=mesh, in_specs=placed, out_specs=P(("out", "inp"), None), check_vma=False
    )
```

```python
import functools

import jax
import jax.numpy as jnp
from jax import lax
from jax.experimental import pallas as pl
from jax.experimental.pallas import tpu as pltpu
from jax.sharding import PartitionSpec as P

LANES = 128
SIDE = 4
CORES = 2
CHUNK = 16
FAR_A = ((2, 0), (3, 1))
FAR_B = ((0, 1), (3, 2))
PAIRS = (
    ((2, 2), (2, 3)), ((2, 0), (2, 1)), ((1, 2), (3, 2)), ((1, 1), (3, 1)),
    ((1, 3), (3, 3)), ((1, 0), (3, 0)), ((0, 2), (0, 1)), ((0, 3), (0, 0)),
)
ARRIVALS = (
    (0, 0), (1, 0), (0, 1), (3, 0), (0, 3), (1, 1),
    (3, 3), (1, 3), (3, 1), (2, 0), (0, 2), (2, 3),
)
LAST = (((3, 2),), ((2, 1), (1, 2), (2, 2)))
ALONG_A, ALONG_B, HOME = range(3)
MESH = pl.DeviceIdType.MESH


def numbers(rows):
    return tuple(sum(row[at] * SIDE**place for place, row in enumerate(rows)) for at in range(len(rows[0])))


def window_of(feats):
    return -(-(CORES * feats + LANES - 1) // LANES) * LANES


def sylvester(order):
    rows = lax.broadcasted_iota(jnp.int32, (order, order), 0)
    cols = lax.broadcasted_iota(jnp.int32, (order, order), 1)
    parity = rows & cols
    for shift in (8, 4, 2, 1):
        parity = parity ^ (parity >> shift)
    return (1 - 2 * (parity & 1)).astype(jnp.float32).astype(jnp.bfloat16)


def identity(order):
    rows = lax.broadcasted_iota(jnp.int32, (order, order), 0)
    cols = lax.broadcasted_iota(jnp.int32, (order, order), 1)
    return jnp.where(rows == cols, 1.0, 0.0).astype(jnp.bfloat16)


def butterfly(values):
    values = list(values)
    stride = 1
    while stride < len(values):
        for at in range(len(values)):
            if at & stride == 0:
                first, second = values[at], values[at + stride]
                values[at], values[at + stride] = first + second, first - second
        stride *= 2
    return values


def exchange_kernel(
    update_hbm, work_ref, update, early, eye, sending, middle, relay, received,
    load_sem, early_sems, send_sems, middle_sems, relay_sems, recv_sems,
):
    cols = update.shape[1]
    stacked = received.shape[1]
    feats = stacked // 2
    groups = cols // feats
    window = window_of(feats)
    me = lax.axis_index("inp")
    core = me % CORES
    my_chip = me // CORES
    my_x = my_chip % SIDE
    my_y = my_chip // SIDE
    my_a = my_x + core * (my_y - my_x)
    my_b = my_y + core * (my_x - my_y)

    def chip_at(da, db):
        a, b = lax.rem(my_a + da, SIDE), lax.rem(my_b + db, SIDE)
        x, y = a + core * (b - a), b + core * (a - b)
        return y * SIDE + x

    firsts_of_chips = [[chip_at(da, db) * CORES for db in range(SIDE)] for da in range(SIDE)]

    def device_at(da, db, c):
        return firsts_of_chips[da % SIDE][db % SIDE] + c

    def window_at(da, db):
        chip = chip_at(da, db)
        first = jnp.minimum(chip * CORES * feats // LANES, (cols - window) // LANES)
        return pl.ds(pl.multiple_of(first * LANES, LANES), window), chip * CORES * feats - first * LANES

    firsts = [
        pltpu.make_async_copy(update_hbm.at[:, window_at(*PAIRS[0][way])[0]], early.at[way], early_sems.at[way])
        for way in range(2)
    ]
    load = pltpu.make_async_copy(update_hbm, update, load_sem)
    for copy in (*firsts, load):
        copy.start()
    barrier = pltpu.get_barrier_semaphore()
    others = [device_at(da, db, c) for da, db in ((1, 0), (3, 0), (0, 1), (0, 3)) for c in range(CORES)]
    others.append(device_at(0, 0, 1 - core))
    for device in others:
        pl.semaphore_signal(barrier, inc=1, device_id={"inp": device}, device_id_type=MESH)

    def make(da, db, columns=None):
        at, shift = window_at(da, db)
        turned = lax.dot_general(
            eye[pl.ds(pl.multiple_of(shift, 16), CORES * feats), :],
            update[:, at] if columns is None else columns,
            (((1,), (1,)), ((), ())),
            preferred_element_type=jnp.float32,
        )
        for c in range(CORES):
            rows = turned[c * feats : (c + 1) * feats]
            sending[da, db, c] = jnp.concatenate([rows[:, :LANES], rows[:, LANES:]], axis=0).astype(sending.dtype)

    def send(src, dst, kind, sem, device):
        pltpu.make_async_remote_copy(
            src_ref=src, dst_ref=dst, send_sem=send_sems.at[kind], recv_sem=sem,
            device_id={"inp": device}, device_id_type=MESH,
        ).start()

    def wait(dst, sem):
        pltpu.make_async_remote_copy(
            src_ref=dst, dst_ref=dst, send_sem=send_sems.at[0], recv_sem=sem,
            device_id={"inp": me}, device_id_type=MESH,
        ).wait_recv()

    def wait_sent(kind, sent):
        pltpu.make_async_remote_copy(
            src_ref=sent, dst_ref=sent, send_sem=send_sems.at[kind], recv_sem=send_sems.at[kind],
            device_id={"inp": me}, device_id_type=MESH,
        ).wait_send()

    def held(da, db):
        return sending.at[da, db] if da == 0 else middle.at[da, db]

    def wait_held(da, db):
        if da != 0:
            wait(middle.at[da, db], middle_sems.at[da, db])

    def to_middle(src, step, da, db):
        send(src, middle.at[da, db], ALONG_A, middle_sems.at[da, db], device_at(step, 0, core))

    def to_relay(src, way, slot):
        step = (1, 3)[way % 2]
        da, db = (step, 0) if way < 2 else (0, step)
        send(src, relay.at[way, slot], way // 2, relay_sems.at[way, slot], device_at(da, db, core))

    def to_ends(blocks):
        for c in range(CORES):
            for src, step, da, db in blocks:
                source = device_at(SIDE - da, db, core)
                send(src.at[c], received.at[source], ALONG_B, recv_sems.at[source], device_at(0, step, c))

    def far_a(slot):
        for way in range(2):
            to_relay(sending.at[2, FAR_A[way][slot]], way, slot)

    def near_a(db):
        for da in (1, 3):
            to_middle(sending.at[da, db], da, da, db)

    def far_b(slot):
        for way in (2, 3):
            wait_held(FAR_B[way - 2][slot], 2)
        for way in (2, 3):
            to_relay(held(FAR_B[way - 2][slot], 2), way, slot)

    def near_b(da):
        for db in (1, 3):
            wait_held(da, db)
        to_ends([(held(da, db), db, da, 0) for db in (1, 3)])

    def on_a(slot):
        for way in range(2):
            wait(relay.at[way, slot], relay_sems.at[way, slot])
            to_middle(relay.at[way, slot], (1, 3)[way], 2, FAR_A[way][slot])

    def on_b(slot):
        for way in (2, 3):
            wait(relay.at[way, slot], relay_sems.at[way, slot])
        to_ends([(relay.at[way, slot], step, FAR_B[way - 2][slot], SIDE - step) for way, step in ((2, 1), (3, 3))])

    def home(da):
        wait_held(da, 0)
        block = held(da, 0)
        source = device_at(SIDE - da, 0, core)
        send(block.at[1 - core], received.at[source], HOME, recv_sems.at[source], device_at(0, 0, 1 - core))
        received[source] = block[core]

    eye[...] = identity(window)
    for way in range(2):
        firsts[way].wait()
    for way in range(2):
        make(*PAIRS[0][way], early[way])
    pl.semaphore_wait(barrier, len(others))
    far_a(0)
    load.wait()

    def second():
        far_a(1)

    def third():
        near_a(2)

    def fourth():
        near_a(1)
        on_a(0)

    def fifth():
        near_a(3)
        on_a(1)

    def sixth():
        near_a(0)

    def seventh():
        far_b(0)

    def make_pair(pair, digits):
        for at in range(2):
            make(digits[2 * at] % SIDE, digits[2 * at + 1] % SIDE)
        for at, action in enumerate((second, third, fourth, fifth, sixth, seventh)):
            pl.when(pair == at)(action)
        return tuple(digit // SIDE for digit in digits)

    lax.fori_loop(0, len(PAIRS) - 1, make_pair, numbers([one + other for one, other in PAIRS[1:]]))
    near_b(0)
    far_b(1)
    near_b(1)
    near_b(3)
    home(0)
    on_b(0)
    near_b(2)
    for da in (1, 3, 2):
        home(da)
    on_b(1)

    matrix = sylvester(2 * LANES)
    factor = 1.0 / jnp.sqrt(jnp.float32(groups * 2 * LANES))

    def rotate(*chips):
        places = []
        for x, y in chips:
            places.append((lax.rem(my_x + SIDE - x, SIDE), lax.rem(my_y + SIDE - y, SIDE)))
            first = (places[-1][1] * SIDE + places[-1][0]) * CORES
            for c, other in enumerate((y + core, x + 1 - core)):

                @pl.when(other > 0)
                def _(source=first + c):
                    wait(received.at[source], recv_sems.at[source])

        for from_x, from_y in places:
            first = (from_y * SIDE + from_x) * CORES
            pair = jnp.concatenate([received[first], received[first + 1]], axis=1)
            both = jnp.dot(pair, matrix, preferred_element_type=jnp.float32)
            low, high = both[:feats], both[feats:]
            for half, value in enumerate((low + high, low - high)):
                for c in range(CORES):
                    work_ref[from_y, from_x, 2 * c + half] = value[:, c * LANES : (c + 1) * LANES] * factor

    def rotate_pair(_, digits):
        rotate(*((digits[2 * at] % SIDE, digits[2 * at + 1] % SIDE) for at in range(2)))
        return tuple(digit // SIDE for digit in digits)

    pairs = [one + other for one, other in zip(ARRIVALS[::2], ARRIVALS[1::2])]
    lax.fori_loop(0, len(pairs), rotate_pair, numbers(pairs))
    wait_sent(ALONG_A, sending)
    wait_sent(HOME, received.at[pl.ds(0, SIDE)])
    for chips in LAST:
        rotate(*chips)
    wait_sent(ALONG_B, sending)


def finish_kernel(work_ref, resident, out_hbm, out, out_sems):
    feats, width = out.shape
    whole = feats // CHUNK

    def store(chunk, rows):
        return pltpu.make_async_copy(out.at[rows], out_hbm.at[rows], out_sems.at[chunk])

    def finish(rows):
        for at in range(2 * CORES):
            values = butterfly([work_ref[y, x, at, rows, :] for y in range(SIDE) for x in range(SIDE)])
            for chip, value in enumerate(values):
                cols = pl.ds((chip * 2 * CORES + at) * LANES, LANES)
                total = resident[rows, cols].astype(jnp.float32) + value
                out[rows, cols] = total.astype(out.dtype)

    @pl.loop(0, whole)
    def _(chunk):
        rows = pl.ds(pl.multiple_of(chunk * CHUNK, CHUNK), CHUNK)
        finish(rows)
        store(chunk, rows).start()

    rest = pl.ds(whole * CHUNK, feats % CHUNK)
    if feats % CHUNK:
        finish(rest)
        store(whole, rest).start()
        store(whole, rest).wait()

    @pl.loop(0, whole)
    def _(chunk):
        store(chunk, pl.ds(pl.multiple_of(chunk * CHUNK, CHUNK), CHUNK)).wait()


def shards(weight_delta, resident):
    rows, cols = weight_delta.shape
    groups = lax.axis_size("inp")
    feats = cols // groups
    size = rows * cols
    work = pl.pallas_call(
        exchange_kernel,
        out_shape=pltpu.VMEM((SIDE, SIDE, 2 * CORES, feats, LANES), jnp.float32),
        in_specs=[pl.BlockSpec(memory_space=pl.ANY)],
        out_specs=pl.BlockSpec(memory_space=pltpu.VMEM),
        scratch_shapes=[
            pltpu.VMEM((rows, cols), weight_delta.dtype),
            pltpu.VMEM((2, rows, window_of(feats)), weight_delta.dtype),
            pltpu.VMEM((window_of(feats), window_of(feats)), weight_delta.dtype),
            pltpu.VMEM((SIDE, SIDE, CORES, 2 * feats, LANES), weight_delta.dtype),
            pltpu.VMEM((SIDE, SIDE, CORES, 2 * feats, LANES), weight_delta.dtype),
            pltpu.VMEM((4, 2, CORES, 2 * feats, LANES), weight_delta.dtype),
            pltpu.VMEM((groups, 2 * feats, LANES), weight_delta.dtype),
            pltpu.SemaphoreType.DMA,
            pltpu.SemaphoreType.DMA((2,)),
            pltpu.SemaphoreType.DMA((3,)),
            pltpu.SemaphoreType.DMA((SIDE, SIDE)),
            pltpu.SemaphoreType.DMA((4, 2)),
            pltpu.SemaphoreType.DMA((groups,)),
        ],
        compiler_params=pltpu.CompilerParams(
            collective_id=0, has_side_effects=True, vmem_limit_bytes=32 * 1024 * 1024
        ),
        cost_estimate=pl.CostEstimate(flops=2 * size * (rows + LANES), bytes_accessed=2 * size, transcendentals=0),
    )(pltpu.with_memory_space_constraint(weight_delta, pltpu.HBM))
    return pl.pallas_call(
        finish_kernel,
        out_shape=jax.ShapeDtypeStruct(resident.shape, resident.dtype),
        in_specs=[pl.BlockSpec(memory_space=pltpu.VMEM)] * 2,
        out_specs=pl.BlockSpec(memory_space=pl.ANY),
        scratch_shapes=[
            pltpu.VMEM(resident.shape, resident.dtype),
            pltpu.SemaphoreType.DMA((-(-feats // CHUNK),)),
        ],
        compiler_params=pltpu.CompilerParams(vmem_limit_bytes=32 * 1024 * 1024),
        cost_estimate=pl.CostEstimate(flops=6 * size, bytes_accessed=4 * size, transcendentals=0),
    )(work, resident)


def solution(mesh):
    placed = (P("inp", "out"), P(("out", "inp"), None))
    return jax.shard_map(
        shards, mesh=mesh, in_specs=placed, out_specs=P(("out", "inp"), None), check_vma=False
    )
```

```python
import functools

import jax
import jax.numpy as jnp
from jax import lax
from jax.experimental import pallas as pl
from jax.experimental.pallas import tpu as pltpu
from jax.sharding import PartitionSpec as P

LANES = 128
SIDE = 4
CORES = 2
CHUNK = 16
FAR_A = ((2, 0), (3, 1))
FAR_B = ((0, 1), (3, 2))
PAIRS = (
    ((2, 2), (2, 3)), ((2, 0), (2, 1)), ((1, 2), (3, 2)), ((1, 1), (3, 1)),
    ((1, 3), (3, 3)), ((1, 0), (3, 0)), ((0, 2), (0, 1)), ((0, 3), (0, 0)),
)
ARRIVALS = (
    (0, 0), (1, 0), (0, 1), (3, 0), (0, 3), (1, 1),
    (3, 3), (1, 3), (3, 1), (2, 0), (0, 2), (2, 3),
)
LAST = (((3, 2),), ((2, 1), (1, 2), (2, 2)))
ALONG_A, ALONG_B, HOME = range(3)
MESH = pl.DeviceIdType.MESH


def numbers(rows):
    return tuple(sum(row[at] * SIDE**place for place, row in enumerate(rows)) for at in range(len(rows[0])))


def window_of(feats):
    return -(-(CORES * feats + LANES - 1) // LANES) * LANES


def sylvester(order):
    rows = lax.broadcasted_iota(jnp.int32, (order, order), 0)
    cols = lax.broadcasted_iota(jnp.int32, (order, order), 1)
    parity = rows & cols
    for shift in (8, 4, 2, 1):
        parity = parity ^ (parity >> shift)
    return (1 - 2 * (parity & 1)).astype(jnp.float32).astype(jnp.bfloat16)


def identity(order):
    rows = lax.broadcasted_iota(jnp.int32, (order, order), 0)
    cols = lax.broadcasted_iota(jnp.int32, (order, order), 1)
    return jnp.where(rows == cols, 1.0, 0.0).astype(jnp.bfloat16)


def butterfly(values):
    values = list(values)
    stride = 1
    while stride < len(values):
        for at in range(len(values)):
            if at & stride == 0:
                first, second = values[at], values[at + stride]
                values[at], values[at + stride] = first + second, first - second
        stride *= 2
    return values


def exchange_kernel(
    update_hbm, work_ref, update, early, eye, sending, middle, relay, received,
    load_sem, early_sems, send_sems, middle_sems, relay_sems, recv_sems,
):
    cols = update.shape[1]
    stacked = received.shape[1]
    feats = stacked // 2
    groups = cols // feats
    window = window_of(feats)
    me = lax.axis_index("inp")
    core = me % CORES
    my_chip = me // CORES
    my_x = my_chip % SIDE
    my_y = my_chip // SIDE
    my_a = my_x + core * (my_y - my_x)
    my_b = my_y + core * (my_x - my_y)

    def chip_at(da, db):
        a, b = lax.rem(my_a + da, SIDE), lax.rem(my_b + db, SIDE)
        x, y = a + core * (b - a), b + core * (a - b)
        return y * SIDE + x

    firsts_of_chips = [[chip_at(da, db) * CORES for db in range(SIDE)] for da in range(SIDE)]

    def device_at(da, db, c):
        return firsts_of_chips[da % SIDE][db % SIDE] + c

    def window_at(da, db):
        chip = chip_at(da, db)
        first = jnp.minimum(chip * CORES * feats // LANES, (cols - window) // LANES)
        return pl.ds(pl.multiple_of(first * LANES, LANES), window), chip * CORES * feats - first * LANES

    firsts = [
        pltpu.make_async_copy(update_hbm.at[:, window_at(*PAIRS[0][way])[0]], early.at[way], early_sems.at[way])
        for way in range(2)
    ]
    load = pltpu.make_async_copy(update_hbm, update, load_sem)
    for copy in (*firsts, load):
        copy.start()
    barrier = pltpu.get_barrier_semaphore()
    others = [device_at(da, db, c) for da, db in ((1, 0), (3, 0), (0, 1), (0, 3)) for c in range(CORES)]
    others.append(device_at(0, 0, 1 - core))
    for device in others:
        pl.semaphore_signal(barrier, inc=1, device_id={"inp": device}, device_id_type=MESH)

    def make(da, db, columns=None):
        at, shift = window_at(da, db)
        turned = lax.dot_general(
            eye[pl.ds(pl.multiple_of(shift, 16), CORES * feats), :],
            update[:, at] if columns is None else columns,
            (((1,), (1,)), ((), ())),
            preferred_element_type=jnp.float32,
        )
        for c in range(CORES):
            rows = turned[c * feats : (c + 1) * feats]
            sending[da, db, c] = jnp.concatenate([rows[:, :LANES], rows[:, LANES:]], axis=0).astype(sending.dtype)

    def send(src, dst, kind, sem, device):
        pltpu.make_async_remote_copy(
            src_ref=src, dst_ref=dst, send_sem=send_sems.at[kind], recv_sem=sem,
            device_id={"inp": device}, device_id_type=MESH,
        ).start()

    def wait(dst, sem):
        pltpu.make_async_remote_copy(
            src_ref=dst, dst_ref=dst, send_sem=send_sems.at[0], recv_sem=sem,
            device_id={"inp": me}, device_id_type=MESH,
        ).wait_recv()

    def wait_sent(kind, sent):
        pltpu.make_async_remote_copy(
            src_ref=sent, dst_ref=sent, send_sem=send_sems.at[kind], recv_sem=send_sems.at[kind],
            device_id={"inp": me}, device_id_type=MESH,
        ).wait_send()

    def held(da, db):
        return sending.at[da, db] if da == 0 else middle.at[da, db]

    def wait_held(da, db):
        if da != 0:
            wait(middle.at[da, db], middle_sems.at[da, db])

    def to_middle(src, step, da, db):
        send(src, middle.at[da, db], ALONG_A, middle_sems.at[da, db], device_at(step, 0, core))

    def to_relay(src, way, slot):
        step = (1, 3)[way % 2]
        da, db = (step, 0) if way < 2 else (0, step)
        send(src, relay.at[way, slot], way // 2, relay_sems.at[way, slot], device_at(da, db, core))

    def to_ends(blocks):
        for c in range(CORES):
            for src, step, da, db in blocks:
                source = device_at(SIDE - da, db, core)
                send(src.at[c], received.at[source], ALONG_B, recv_sems.at[source], device_at(0, step, c))

    def far_a(slot):
        for way in range(2):
            to_relay(sending.at[2, FAR_A[way][slot]], way, slot)

    def near_a(db):
        for da in (1, 3):
            to_middle(sending.at[da, db], da, da, db)

    def far_b(slot):
        for way in (2, 3):
            wait_held(FAR_B[way - 2][slot], 2)
        for way in (2, 3):
            to_relay(held(FAR_B[way - 2][slot], 2), way, slot)

    def near_b(da):
        for db in (1, 3):
            wait_held(da, db)
        to_ends([(held(da, db), db, da, 0) for db in (1, 3)])

    def on_a(slot):
        for way in range(2):
            wait(relay.at[way, slot], relay_sems.at[way, slot])
            to_middle(relay.at[way, slot], (1, 3)[way], 2, FAR_A[way][slot])

    def on_b(slot):
        for way in (2, 3):
            wait(relay.at[way, slot], relay_sems.at[way, slot])
        to_ends([(relay.at[way, slot], step, FAR_B[way - 2][slot], SIDE - step) for way, step in ((2, 1), (3, 3))])

    def home(da):
        wait_held(da, 0)
        block = held(da, 0)
        source = device_at(SIDE - da, 0, core)
        send(block.at[1 - core], received.at[source], HOME, recv_sems.at[source], device_at(0, 0, 1 - core))
        received[source] = block[core]

    eye[...] = identity(window)
    for way in range(2):
        firsts[way].wait()
    for way in range(2):
        make(*PAIRS[0][way], early[way])
    pl.semaphore_wait(barrier, len(others))
    far_a(0)
    load.wait()

    def second():
        far_a(1)

    def third():
        near_a(2)

    def fourth():
        near_a(1)
        on_a(0)

    def fifth():
        near_a(3)
        on_a(1)

    def sixth():
        near_a(0)

    def seventh():
        far_b(0)

    def make_pair(pair, digits):
        for at in range(2):
            make(digits[2 * at] % SIDE, digits[2 * at + 1] % SIDE)
        for at, action in enumerate((second, third, fourth, fifth, sixth, seventh)):
            pl.when(pair == at)(action)
        return tuple(digit // SIDE for digit in digits)

    lax.fori_loop(0, len(PAIRS) - 1, make_pair, numbers([one + other for one, other in PAIRS[1:]]))
    near_b(0)
    far_b(1)
    near_b(1)
    near_b(3)
    home(0)
    on_b(0)
    near_b(2)
    for da in (1, 3, 2):
        home(da)
    on_b(1)

    matrix = sylvester(2 * LANES)
    factor = 1.0 / jnp.sqrt(jnp.float32(groups * 2 * LANES))

    def rotate(*chips):
        places = []
        for x, y in chips:
            places.append((lax.rem(my_x + SIDE - x, SIDE), lax.rem(my_y + SIDE - y, SIDE)))
            first = (places[-1][1] * SIDE + places[-1][0]) * CORES
            for c, other in enumerate((y + core, x + 1 - core)):

                @pl.when(other > 0)
                def _(source=first + c):
                    wait(received.at[source], recv_sems.at[source])

        for from_x, from_y in places:
            first = (from_y * SIDE + from_x) * CORES
            pair = jnp.concatenate([received[first], received[first + 1]], axis=1)
            both = jnp.dot(pair, matrix, preferred_element_type=jnp.float32)
            low, high = both[:feats], both[feats:]
            for half, value in enumerate((low + high, low - high)):
                for c in range(CORES):
                    work_ref[from_y, from_x, 2 * c + half] = value[:, c * LANES : (c + 1) * LANES] * factor

    def rotate_pair(_, digits):
        rotate(*((digits[2 * at] % SIDE, digits[2 * at + 1] % SIDE) for at in range(2)))
        return tuple(digit // SIDE for digit in digits)

    pairs = [one + other for one, other in zip(ARRIVALS[::2], ARRIVALS[1::2])]
    lax.fori_loop(0, len(pairs), rotate_pair, numbers(pairs))
    wait_sent(ALONG_A, sending)
    wait_sent(HOME, received.at[pl.ds(0, SIDE)])
    for chips in LAST:
        rotate(*chips)
    wait_sent(ALONG_B, sending)


def finish_kernel(work_ref, resident, out_hbm, out, out_sem):
    feats, width = out.shape
    chips = SIDE * SIDE
    whole = feats // CHUNK

    def finish(core, rows):
        for at in (2 * core, 2 * core + 1):
            values = butterfly([work_ref[y, x, at, rows, :] for y in range(SIDE) for x in range(SIDE)])
            for chip, value in enumerate(values):
                cols = pl.ds((chip * 2 * CORES + at) * LANES, LANES)
                total = resident[rows, cols].astype(jnp.float32) + value
                out[rows, cols] = total.astype(out.dtype)

    for core in range(CORES):

        @pl.loop(0, whole)
        def _(chunk, core=core):
            finish(core, pl.ds(pl.multiple_of(chunk * CHUNK, CHUNK), CHUNK))

        if feats % CHUNK:
            finish(core, pl.ds(whole * CHUNK, feats % CHUNK))
        for chip in range(chips):
            cols = pl.ds((chip * CORES + core) * 2 * LANES, 2 * LANES)
            pltpu.make_async_copy(out.at[:, cols], out_hbm.at[:, cols], out_sem).start()
    pltpu.make_async_copy(out, out_hbm, out_sem).wait()


def shards(weight_delta, resident):
    rows, cols = weight_delta.shape
    groups = lax.axis_size("inp")
    feats = cols // groups
    size = rows * cols
    work = pl.pallas_call(
        exchange_kernel,
        out_shape=pltpu.VMEM((SIDE, SIDE, 2 * CORES, feats, LANES), jnp.float32),
        in_specs=[pl.BlockSpec(memory_space=pl.ANY)],
        out_specs=pl.BlockSpec(memory_space=pltpu.VMEM),
        scratch_shapes=[
            pltpu.VMEM((rows, cols), weight_delta.dtype),
            pltpu.VMEM((2, rows, window_of(feats)), weight_delta.dtype),
            pltpu.VMEM((window_of(feats), window_of(feats)), weight_delta.dtype),
            pltpu.VMEM((SIDE, SIDE, CORES, 2 * feats, LANES), weight_delta.dtype),
            pltpu.VMEM((SIDE, SIDE, CORES, 2 * feats, LANES), weight_delta.dtype),
            pltpu.VMEM((4, 2, CORES, 2 * feats, LANES), weight_delta.dtype),
            pltpu.VMEM((groups, 2 * feats, LANES), weight_delta.dtype),
            pltpu.SemaphoreType.DMA,
            pltpu.SemaphoreType.DMA((2,)),
            pltpu.SemaphoreType.DMA((3,)),
            pltpu.SemaphoreType.DMA((SIDE, SIDE)),
            pltpu.SemaphoreType.DMA((4, 2)),
            pltpu.SemaphoreType.DMA((groups,)),
        ],
        compiler_params=pltpu.CompilerParams(
            collective_id=0, has_side_effects=True, vmem_limit_bytes=32 * 1024 * 1024
        ),
        cost_estimate=pl.CostEstimate(flops=2 * size * (rows + LANES), bytes_accessed=2 * size, transcendentals=0),
    )(pltpu.with_memory_space_constraint(weight_delta, pltpu.HBM))
    return pl.pallas_call(
        finish_kernel,
        out_shape=jax.ShapeDtypeStruct(resident.shape, resident.dtype),
        in_specs=[pl.BlockSpec(memory_space=pltpu.VMEM)] * 2,
        out_specs=pl.BlockSpec(memory_space=pl.ANY),
        scratch_shapes=[
            pltpu.VMEM(resident.shape, resident.dtype),
            pltpu.SemaphoreType.DMA,
        ],
        compiler_params=pltpu.CompilerParams(vmem_limit_bytes=32 * 1024 * 1024),
        cost_estimate=pl.CostEstimate(flops=6 * size, bytes_accessed=4 * size, transcendentals=0),
    )(work, resident)


def solution(mesh):
    placed = (P("inp", "out"), P(("out", "inp"), None))
    return jax.shard_map(
        shards, mesh=mesh, in_specs=placed, out_specs=P(("out", "inp"), None), check_vma=False
    )
```

```python
import functools

import jax
import jax.numpy as jnp
from jax import lax
from jax.experimental import pallas as pl
from jax.experimental.pallas import tpu as pltpu
from jax.sharding import PartitionSpec as P

LANES = 128
SIDE = 4
CORES = 2
CHUNK = 16
FAR_A = ((2, 0), (3, 1))
FAR_B = ((0, 1), (3, 2))
PAIRS = (
    ((2, 2), (2, 3)), ((2, 0), (2, 1)), ((1, 2), (3, 2)), ((1, 1), (3, 1)),
    ((1, 3), (3, 3)), ((1, 0), (3, 0)), ((0, 2), (0, 1)), ((0, 3), (0, 0)),
)
ARRIVALS = (
    (0, 0), (1, 0), (0, 1), (3, 0), (0, 3), (1, 1),
    (3, 3), (1, 3), (3, 1), (2, 0), (0, 2), (2, 3),
)
LAST = (((3, 2),), ((2, 1), (1, 2), (2, 2)))
ALONG_A, ALONG_B, HOME = range(3)
MESH = pl.DeviceIdType.MESH


def numbers(rows):
    return tuple(sum(row[at] * SIDE**place for place, row in enumerate(rows)) for at in range(len(rows[0])))


def window_of(feats):
    return -(-(CORES * feats + LANES - 1) // LANES) * LANES


def sylvester(order):
    rows = lax.broadcasted_iota(jnp.int32, (order, order), 0)
    cols = lax.broadcasted_iota(jnp.int32, (order, order), 1)
    parity = rows & cols
    for shift in (8, 4, 2, 1):
        parity = parity ^ (parity >> shift)
    return (1 - 2 * (parity & 1)).astype(jnp.float32).astype(jnp.bfloat16)


def identity(order):
    rows = lax.broadcasted_iota(jnp.int32, (order, order), 0)
    cols = lax.broadcasted_iota(jnp.int32, (order, order), 1)
    return jnp.where(rows == cols, 1.0, 0.0).astype(jnp.bfloat16)


def butterfly(values):
    values = list(values)
    stride = 1
    while stride < len(values):
        for at in range(len(values)):
            if at & stride == 0:
                first, second = values[at], values[at + stride]
                values[at], values[at + stride] = first + second, first - second
        stride *= 2
    return values


def exchange_kernel(
    update_hbm, work_ref, update, early, eye, sending, middle, relay, received,
    load_sem, early_sems, send_sems, middle_sems, relay_sems, recv_sems,
):
    cols = update.shape[1]
    stacked = received.shape[1]
    feats = stacked // 2
    groups = cols // feats
    window = window_of(feats)
    me = lax.axis_index("inp")
    core = me % CORES
    my_chip = me // CORES
    my_x = my_chip % SIDE
    my_y = my_chip // SIDE
    my_a = my_x + core * (my_y - my_x)
    my_b = my_y + core * (my_x - my_y)

    def chip_at(da, db):
        a, b = lax.rem(my_a + da, SIDE), lax.rem(my_b + db, SIDE)
        x, y = a + core * (b - a), b + core * (a - b)
        return y * SIDE + x

    firsts_of_chips = [[chip_at(da, db) * CORES for db in range(SIDE)] for da in range(SIDE)]

    def device_at(da, db, c):
        return firsts_of_chips[da % SIDE][db % SIDE] + c

    def window_at(da, db):
        chip = chip_at(da, db)
        first = jnp.minimum(chip * CORES * feats // LANES, (cols - window) // LANES)
        return pl.ds(pl.multiple_of(first * LANES, LANES), window), chip * CORES * feats - first * LANES

    firsts = [
        pltpu.make_async_copy(update_hbm.at[:, window_at(*PAIRS[0][way])[0]], early.at[way], early_sems.at[way])
        for way in range(2)
    ]
    load = pltpu.make_async_copy(update_hbm, update, load_sem)
    for copy in (*firsts, load):
        copy.start()
    barrier = pltpu.get_barrier_semaphore()
    others = [device_at(da, db, c) for da, db in ((1, 0), (3, 0), (0, 1), (0, 3)) for c in range(CORES)]
    others.append(device_at(0, 0, 1 - core))
    for device in others:
        pl.semaphore_signal(barrier, inc=1, device_id={"inp": device}, device_id_type=MESH)

    def make(da, db, columns=None):
        at, shift = window_at(da, db)
        turned = lax.dot_general(
            eye[pl.ds(pl.multiple_of(shift, 16), CORES * feats), :],
            update[:, at] if columns is None else columns,
            (((1,), (1,)), ((), ())),
            preferred_element_type=jnp.float32,
        )
        for c in range(CORES):
            rows = turned[c * feats : (c + 1) * feats]
            sending[da, db, c] = jnp.concatenate([rows[:, :LANES], rows[:, LANES:]], axis=0).astype(sending.dtype)

    def send(src, dst, kind, sem, device):
        pltpu.make_async_remote_copy(
            src_ref=src, dst_ref=dst, send_sem=send_sems.at[kind], recv_sem=sem,
            device_id={"inp": device}, device_id_type=MESH,
        ).start()

    def wait(dst, sem):
        pltpu.make_async_remote_copy(
            src_ref=dst, dst_ref=dst, send_sem=send_sems.at[0], recv_sem=sem,
            device_id={"inp": me}, device_id_type=MESH,
        ).wait_recv()

    def wait_sent(kind, sent):
        pltpu.make_async_remote_copy(
            src_ref=sent, dst_ref=sent, send_sem=send_sems.at[kind], recv_sem=send_sems.at[kind],
            device_id={"inp": me}, device_id_type=MESH,
        ).wait_send()

    def held(da, db):
        return sending.at[da, db] if da == 0 else middle.at[da, db]

    def wait_held(da, db):
        if da != 0:
            wait(middle.at[da, db], middle_sems.at[da, db])

    def to_middle(src, step, da, db):
        send(src, middle.at[da, db], ALONG_A, middle_sems.at[da, db], device_at(step, 0, core))

    def to_relay(src, way, slot):
        step = (1, 3)[way % 2]
        da, db = (step, 0) if way < 2 else (0, step)
        send(src, relay.at[way, slot], way // 2, relay_sems.at[way, slot], device_at(da, db, core))

    def to_ends(blocks):
        for c in range(CORES):
            for src, step, da, db in blocks:
                source = device_at(SIDE - da, db, core)
                send(src.at[c], received.at[source], ALONG_B, recv_sems.at[source], device_at(0, step, c))

    def far_a(slot):
        for way in range(2):
            to_relay(sending.at[2, FAR_A[way][slot]], way, slot)

    def near_a(db):
        for da in (1, 3):
            to_middle(sending.at[da, db], da, da, db)

    def far_b(slot):
        for way in (2, 3):
            wait_held(FAR_B[way - 2][slot], 2)
        for way in (2, 3):
            to_relay(held(FAR_B[way - 2][slot], 2), way, slot)

    def near_b(da):
        for db in (1, 3):
            wait_held(da, db)
        to_ends([(held(da, db), db, da, 0) for db in (1, 3)])

    def on_a(slot):
        for way in range(2):
            wait(relay.at[way, slot], relay_sems.at[way, slot])
            to_middle(relay.at[way, slot], (1, 3)[way], 2, FAR_A[way][slot])

    def on_b(slot):
        for way in (2, 3):
            wait(relay.at[way, slot], relay_sems.at[way, slot])
        to_ends([(relay.at[way, slot], step, FAR_B[way - 2][slot], SIDE - step) for way, step in ((2, 1), (3, 3))])

    def home(da):
        wait_held(da, 0)
        block = held(da, 0)
        source = device_at(SIDE - da, 0, core)
        send(block.at[1 - core], received.at[source], HOME, recv_sems.at[source], device_at(0, 0, 1 - core))
        received[source] = block[core]

    eye[...] = identity(window)
    for way in range(2):
        firsts[way].wait()
    for way in range(2):
        make(*PAIRS[0][way], early[way])
    pl.semaphore_wait(barrier, len(others))
    far_a(0)
    load.wait()

    def second():
        far_a(1)

    def third():
        near_a(2)

    def fourth():
        near_a(1)
        on_a(0)

    def fifth():
        near_a(3)
        on_a(1)

    def sixth():
        near_a(0)

    def seventh():
        far_b(0)

    def make_pair(pair, digits):
        for at in range(2):
            make(digits[2 * at] % SIDE, digits[2 * at + 1] % SIDE)
        for at, action in enumerate((second, third, fourth, fifth, sixth, seventh)):
            pl.when(pair == at)(action)
        return tuple(digit // SIDE for digit in digits)

    lax.fori_loop(0, len(PAIRS) - 1, make_pair, numbers([one + other for one, other in PAIRS[1:]]))
    near_b(0)
    far_b(1)
    near_b(1)
    near_b(3)
    home(0)
    on_b(0)
    near_b(2)
    for da in (1, 3, 2):
        home(da)
    on_b(1)

    matrix = sylvester(2 * LANES)
    factor = 1.0 / jnp.sqrt(jnp.float32(groups * 2 * LANES))

    def rotate(*chips):
        places = []
        for x, y in chips:
            places.append((lax.rem(my_x + SIDE - x, SIDE), lax.rem(my_y + SIDE - y, SIDE)))
            first = (places[-1][1] * SIDE + places[-1][0]) * CORES
            for c, other in enumerate((y + core, x + 1 - core)):

                @pl.when(other > 0)
                def _(source=first + c):
                    wait(received.at[source], recv_sems.at[source])

        for from_x, from_y in places:
            first = (from_y * SIDE + from_x) * CORES
            pair = jnp.concatenate([received[first], received[first + 1]], axis=1)
            both = jnp.dot(pair, matrix, preferred_element_type=jnp.float32)
            low, high = both[:feats], both[feats:]
            for half, value in enumerate((low + high, low - high)):
                for c in range(CORES):
                    work_ref[from_y, from_x, 2 * c + half] = value[:, c * LANES : (c + 1) * LANES] * factor

    def rotate_pair(_, digits):
        rotate(*((digits[2 * at] % SIDE, digits[2 * at + 1] % SIDE) for at in range(2)))
        return tuple(digit // SIDE for digit in digits)

    pairs = [one + other for one, other in zip(ARRIVALS[::2], ARRIVALS[1::2])]
    lax.fori_loop(0, len(pairs), rotate_pair, numbers(pairs))
    wait_sent(ALONG_A, sending)
    wait_sent(HOME, received.at[pl.ds(0, SIDE)])
    for chips in LAST:
        rotate(*chips)
    wait_sent(ALONG_B, sending)


def finish_kernel(work_ref, resident, out_hbm, out, out_sem):
    feats, width = out.shape
    chips = SIDE * SIDE
    whole = feats // CHUNK

    def finish(group, rows):
        for at in group:
            values = butterfly([work_ref[y, x, at, rows, :] for y in range(SIDE) for x in range(SIDE)])
            for chip, value in enumerate(values):
                cols = pl.ds((chip * 2 * CORES + at) * LANES, LANES)
                total = resident[rows, cols].astype(jnp.float32) + value
                out[rows, cols] = total.astype(out.dtype)

    for group in ((0, 1), (2,), (3,)):

        @pl.loop(0, whole)
        def _(chunk, group=group):
            finish(group, pl.ds(pl.multiple_of(chunk * CHUNK, CHUNK), CHUNK))

        if feats % CHUNK:
            finish(group, pl.ds(whole * CHUNK, feats % CHUNK))
        for chip in range(chips):
            cols = pl.ds((chip * 2 * CORES + group[0]) * LANES, len(group) * LANES)
            pltpu.make_async_copy(out.at[:, cols], out_hbm.at[:, cols], out_sem).start()
    pltpu.make_async_copy(out, out_hbm, out_sem).wait()


def shards(weight_delta, resident):
    rows, cols = weight_delta.shape
    groups = lax.axis_size("inp")
    feats = cols // groups
    size = rows * cols
    work = pl.pallas_call(
        exchange_kernel,
        out_shape=pltpu.VMEM((SIDE, SIDE, 2 * CORES, feats, LANES), jnp.float32),
        in_specs=[pl.BlockSpec(memory_space=pl.ANY)],
        out_specs=pl.BlockSpec(memory_space=pltpu.VMEM),
        scratch_shapes=[
            pltpu.VMEM((rows, cols), weight_delta.dtype),
            pltpu.VMEM((2, rows, window_of(feats)), weight_delta.dtype),
            pltpu.VMEM((window_of(feats), window_of(feats)), weight_delta.dtype),
            pltpu.VMEM((SIDE, SIDE, CORES, 2 * feats, LANES), weight_delta.dtype),
            pltpu.VMEM((SIDE, SIDE, CORES, 2 * feats, LANES), weight_delta.dtype),
            pltpu.VMEM((4, 2, CORES, 2 * feats, LANES), weight_delta.dtype),
            pltpu.VMEM((groups, 2 * feats, LANES), weight_delta.dtype),
            pltpu.SemaphoreType.DMA,
            pltpu.SemaphoreType.DMA((2,)),
            pltpu.SemaphoreType.DMA((3,)),
            pltpu.SemaphoreType.DMA((SIDE, SIDE)),
            pltpu.SemaphoreType.DMA((4, 2)),
            pltpu.SemaphoreType.DMA((groups,)),
        ],
        compiler_params=pltpu.CompilerParams(
            collective_id=0, has_side_effects=True, vmem_limit_bytes=32 * 1024 * 1024
        ),
        cost_estimate=pl.CostEstimate(flops=2 * size * (rows + LANES), bytes_accessed=2 * size, transcendentals=0),
    )(pltpu.with_memory_space_constraint(weight_delta, pltpu.HBM))
    return pl.pallas_call(
        finish_kernel,
        out_shape=jax.ShapeDtypeStruct(resident.shape, resident.dtype),
        in_specs=[pl.BlockSpec(memory_space=pltpu.VMEM)] * 2,
        out_specs=pl.BlockSpec(memory_space=pl.ANY),
        scratch_shapes=[
            pltpu.VMEM(resident.shape, resident.dtype),
            pltpu.SemaphoreType.DMA,
        ],
        compiler_params=pltpu.CompilerParams(vmem_limit_bytes=32 * 1024 * 1024),
        cost_estimate=pl.CostEstimate(flops=6 * size, bytes_accessed=4 * size, transcendentals=0),
    )(work, resident)


def solution(mesh):
    placed = (P("inp", "out"), P(("out", "inp"), None))
    return jax.shard_map(
        shards, mesh=mesh, in_specs=placed, out_specs=P(("out", "inp"), None), check_vma=False
    )
```
